128 devices in a mesh: feed: 4 (over x), freq: 32 (over z, y, core).
Axes of the slice: x: 4, y: 4, z: 4, core: 2. Of those that a mesh axis runs over, the one named last changes fastest.
Arguments:
- voltage: bfloat16 [2, 1024, 131072], P(None, 'feed', 'freq'), may hold values from -6 to 6
- flags: int32 [4, 512], P('feed'), may hold values 0 or 1
- owner_slot: int32 [512], replicated, may hold values from 0 to 639, as said below
Outputs:
- visibility: bfloat16 [640, 2, 1024, 1024], P('freq', None, 'feed')
The draws below stay inside these ranges and needn't reach their ends.
Inputs may be any that keep to these rules, and one draw needn't show every extreme that they name: `owner_slot`: distinct slots; slot s belongs to owner s // 20 of freq. No owner gets more than 20 channels, and some owner gets exactly 20.
All inputs are finite; a program needn't handle non-finite values. No bound on the sum of `flags` on one device may be relied on, other than what follows from the above.
Results may differ from the reference program's by a relative error of at most 0.0073.
Values may be sent and summed in bfloat16 or wider, within the bound.
No kernel may reach another device: no remote copies, remote signals or barrier semaphores. Data moves between devices by JAX's collectives and lax.ppermute only.
A program may use at most 192 MiB of HBM per device.

```python
import math
import jax
import jax.numpy as jnp
from jax import lax

F = 1024
CH = 1024
TAPS = 4
BAND_LO = 256
CAP = 20
BAND = 512
NSPEC = 128
SAMPLES = 131072
N_FEED = 4
N_FREQ = 32


def draw_owner_slot(key, part):
    key = jax.random.fold_in(key, 7)
    first, second, third = jax.random.split(key, 3)
    slot_count = N_FREQ * CAP
    filled = jax.random.randint(first, (), 0, N_FREQ)
    scores = jax.random.permutation(second, slot_count).astype(jnp.int32)
    slot_ids = jnp.arange(slot_count, dtype=jnp.int32)
    scores = jnp.where(slot_ids // CAP == filled, slot_ids - slot_count, scores)
    ordered = jnp.argsort(scores, stable=True)
    chosen = ordered[:BAND]
    return jax.random.permutation(third, chosen).astype(jnp.int32)


def touch_ends(entries, rng, smallest, high):
    extent = entries.shape
    spot = [jax.random.randint(jax.random.fold_in(rng, axis), (), 0, extent[axis]) for axis in range(len(extent))]
    entries = entries.at[tuple(spot)].set(smallest)
    longest = extent.index(max(extent))
    spot[longest] = (spot[longest] + 1) % extent[longest]
    return entries.at[tuple(spot)].set(high)


def block_scale(stream_key, dims, shards, low, largest):
    gain = 1.0
    for dim, shards_of in shards:
        heights = jax.random.uniform(jax.random.fold_in(jax.random.fold_in(stream_key, 6), dim), (shards_of,), jnp.float32, low / len(shards), largest / len(shards))
        gain = gain * jnp.repeat(jnp.exp(heights), dims[dim] // shards_of).reshape((-1,) + (1,) * (len(dims) - 1 - dim))
    return gain


def normal_values(key, shape, deviation, bound, pieces=(), kind=jnp.bfloat16):
    drawn = deviation * jax.random.normal(key, shape, jnp.float32)
    if pieces:
        drawn = drawn * block_scale(key, shape, pieces, -0.22, 0.18)
    return jnp.clip(drawn, -bound, bound).astype(kind)


def setup_inputs(seed: int = 0) -> dict:
    seeds = jax.random.split(jax.random.key(seed), 4)
    return {
        "voltage": normal_values(seeds[0], (2, F, SAMPLES), 1.0, 6.0, ((1, 4), (2, 32))),
        "flags": touch_ends((jax.random.randint(seeds[1], (N_FEED, BAND), 0, 4) < 3).astype(jnp.int32), jax.random.fold_in(seeds[1], 1), 0, 1),
        "owner_slot": draw_owner_slot(jax.random.fold_in(seeds[3], 71), 0),
    }


def prototype():
    total = TAPS * CH
    position = jnp.arange(total, dtype=jnp.int32).astype(jnp.float32)
    offset = (position - total / 2 + 0.5) / CH
    taper = 0.5 - 0.5 * jnp.cos(2 * jnp.pi * (position + 0.5) / total)
    coeffs = jnp.sinc(offset) * taper
    coeffs = coeffs * jnp.sqrt(CH / jnp.sum(coeffs * coeffs))
    return coeffs.reshape(TAPS, CH)

def tables(band):
    sample = jnp.arange(CH, dtype=jnp.int32)
    channel = jnp.arange(band, dtype=jnp.int32) + BAND_LO
    phase = (sample[:, None] * channel[None, :] % CH).astype(jnp.float32) * (2 * jnp.pi / CH)
    return (jnp.cos(phase).astype(jnp.bfloat16), jnp.sin(phase).astype(jnp.bfloat16))

def channelize(voltage, extra, flag_row):
    band = flag_row.shape[0]
    longer = jnp.concatenate([voltage, extra], 2)
    count = voltage.shape[2] // CH
    feeds = voltage.shape[1]
    blocks = longer.reshape(2, feeds, count + TAPS - 1, CH)
    coeffs = prototype()
    summed = blocks[:, :, 0:count, :].astype(jnp.float32) * coeffs[0]
    for tap_index in range(1, TAPS):
        summed = summed + blocks[:, :, tap_index:tap_index + count, :].astype(jnp.float32) * coeffs[tap_index]
    weighted = summed.astype(jnp.bfloat16)
    cosine, sine = tables(band)
    real_rows = weighted[0].reshape(feeds * count, CH)
    imag_rows = weighted[1].reshape(feeds * count, CH)
    real_part = jnp.dot(real_rows, cosine, preferred_element_type=jnp.float32) + jnp.dot(imag_rows, sine, preferred_element_type=jnp.float32)
    imag_part = jnp.dot(imag_rows, cosine, preferred_element_type=jnp.float32) - jnp.dot(real_rows, sine, preferred_element_type=jnp.float32)
    joined = jnp.stack([real_part, imag_part], 0).reshape(2, feeds, count, band)
    joined = joined * (flag_row.astype(jnp.float32) * (1.0 / math.sqrt(CH)))
    return jnp.transpose(joined, (3, 0, 2, 1)).astype(jnp.bfloat16)

def reference(voltage, flags, owner_slot):
    group_feeds = F // N_FEED
    groups = jnp.transpose(voltage.reshape(2, N_FEED, group_feeds, SAMPLES), (1, 0, 2, 3))
    padding = jnp.zeros((N_FEED, 2, group_feeds, (TAPS - 1) * CH), jnp.bfloat16)

    def one_group(bundle):
        return channelize(bundle[0], bundle[1], bundle[2])
    spectra = lax.map(one_group, (groups, padding, flags))
    spectra = jnp.transpose(spectra, (1, 2, 3, 0, 4)).reshape(BAND, 2, NSPEC, F)
    inverse = 1.0 / NSPEC

    def correlate(block):
        wide = block.astype(jnp.float32)
        swapped = jnp.stack([wide[1], -wide[0]], 0)
        real_vis = jnp.einsum('zsf,zsg->fg', wide, wide, precision=lax.Precision.HIGHEST)
        imag_vis = jnp.einsum('zsf,zsg->fg', wide, swapped, precision=lax.Precision.HIGHEST)
        return (jnp.stack([real_vis, imag_vis], 0) * inverse).astype(jnp.bfloat16)
    visible = lax.map(correlate, spectra)
    result = jnp.zeros((N_FREQ * CAP, 2, F, F), jnp.bfloat16)
    return result.at[owner_slot].set(visible)
```

```python
import math

import jax
import jax.numpy as jnp
import ml_dtypes
import numpy as np
from jax import lax
from jax.experimental import pallas as pl
from jax.experimental.pallas import tpu as pltpu
from jax.sharding import PartitionSpec as P

CH = 1024
TAPS = 4
BAND_LO = 256
CAP = 20
CORES = 2
BLOCKS = 4
SPECTRA = 8
CHUNKS = (4, 4, 4, 4, 4)
VMEM = 60 * 1024 * 1024


def prototype():
    total = TAPS * CH
    position = np.arange(total).astype(np.float32)
    offset = (position - total / 2 + 0.5) / CH
    taper = 0.5 - 0.5 * np.cos(2 * np.pi * (position + 0.5) / total)
    coeffs = np.sinc(offset) * taper
    coeffs = coeffs * np.sqrt(CH / np.sum(coeffs * coeffs))
    return coeffs.reshape(TAPS, CH).astype(np.float32)


def tables(band):
    sample = np.arange(CH)
    channel = np.arange(band) + BAND_LO
    phase = (channel[:, None] * sample[None, :] % CH).astype(np.float32) * np.float32(2 * np.pi / CH)
    cosine = np.cos(phase).astype(ml_dtypes.bfloat16)
    sine = np.sin(phase).astype(ml_dtypes.bfloat16)
    return np.concatenate([cosine, sine, -sine, cosine], 1)


def moved(value, axis, pairs):
    return lax.ppermute(value, axis, pairs)


def weigh_kernel(place, voltage, other, after, before, coeffs, out, held, sems):
    core = place[0]
    half = voltage.shape[1] // CORES
    own_rows = pl.ds(pl.multiple_of(core * half, half), half)
    span = BLOCKS * CH
    own_at = pl.ds(pl.multiple_of(CH + core * span, CH), span)
    other_at = pl.ds(pl.multiple_of(CH + (1 - core) * span, CH), span)
    copies = [
        pltpu.make_async_copy(voltage.at[:, own_rows, :], held.at[:, :, own_at], sems.at[0]),
        pltpu.make_async_copy(other, held.at[:, :, other_at], sems.at[1]),
        pltpu.make_async_copy(after, held.at[:, :, pl.ds(CH + 2 * span, 2 * CH)], sems.at[2]),
        pltpu.make_async_copy(before, held.at[:, :, pl.ds(0, CH)], sems.at[3]),
    ]
    for copy in copies:
        copy.start()
    for copy in copies:
        copy.wait()
    keep = place[1].astype(jnp.float32)
    rows = 16
    width = 256

    def step(index, carry):
        at = pl.ds(pl.multiple_of(index * rows, rows), rows)
        for z in range(2):
            for start in range(0, CH, width):
                blocks = [
                    held[z, at, pl.ds(b * CH + start, width)].astype(jnp.float32)
                    for b in range(SPECTRA + TAPS - 1)
                ]
                taps = [coeffs[p : p + 1, pl.ds(start, width)] for p in range(TAPS)]
                for s in range(SPECTRA):
                    total = blocks[s] * taps[0]
                    for p in range(1, TAPS):
                        tap = taps[p] * keep if s == 0 else taps[p]
                        total = total + blocks[s + p] * tap
                    out[s, at, pl.ds(z * CH + start, width)] = total.astype(jnp.bfloat16)
        return carry

    lax.fori_loop(0, half // rows, step, 0)


def weigh(place, voltage, other, after, before):
    half = voltage.shape[1] // CORES
    anywhere = pl.BlockSpec(memory_space=pl.ANY)
    return pl.pallas_call(
        weigh_kernel,
        out_shape=jax.ShapeDtypeStruct((SPECTRA, half, 2 * CH), jnp.bfloat16),
        in_specs=[pl.BlockSpec(memory_space=pltpu.SMEM)]
        + [anywhere] * 4
        + [pl.BlockSpec(memory_space=pltpu.VMEM)],
        out_specs=pl.BlockSpec(memory_space=pltpu.VMEM),
        scratch_shapes=[
            pltpu.VMEM((2, half, (SPECTRA + TAPS - 1) * CH), jnp.bfloat16),
            pltpu.SemaphoreType.DMA((4,)),
        ],
        compiler_params=pltpu.CompilerParams(vmem_limit_bytes=VMEM),
        name="weigh",
    )(place, voltage, other, after, before, jnp.asarray(prototype()))


def transform_kernel(table, weighted, out, held):
    rows = table.shape[0]
    both = jnp.concatenate([table[:, : 2 * CH], table[:, 2 * CH :]], 0)
    half = weighted.shape[1]
    for s in range(0, SPECTRA, 2):
        samples = weighted[pl.ds(s, 2)].reshape(2 * half, 2 * CH)
        product = lax.dot_general(
            both, samples, (((1,), (1,)), ((), ())), preferred_element_type=jnp.float32
        )
        for z in range(2):
            for k in range(2):
                held[pl.ds(z * SPECTRA + s + k, rows, stride=2 * SPECTRA), :] = product[
                    z * rows : (z + 1) * rows, k * half : (k + 1) * half
                ]
    out[...] = held[...].reshape(out.shape).astype(jnp.bfloat16)


def transform(table, weighted):
    rows = table.shape[0]
    half = weighted.shape[1]
    return pl.pallas_call(
        transform_kernel,
        out_shape=jax.ShapeDtypeStruct((rows, 2 * SPECTRA, half), jnp.bfloat16),
        in_specs=[pl.BlockSpec(memory_space=pltpu.VMEM)] * 2,
        out_specs=pl.BlockSpec(memory_space=pltpu.VMEM),
        scratch_shapes=[pltpu.VMEM((rows * 2 * SPECTRA, half), jnp.float32)],
        compiler_params=pltpu.CompilerParams(vmem_limit_bytes=VMEM),
        name="transform",
    )(table, weighted)


def halves(block):
    count, _, rows, lanes = block.shape
    split = block.reshape(count // CORES, CORES, rows, lanes)
    return jnp.concatenate(
        [split[:, core].reshape(count // CORES * rows, lanes) for core in range(CORES)], 1
    )


def correlate_kernel(place, own, left, right, far_low, far_high, *rest):
    out = rest[-1]
    me = place[2]
    group = out.shape[2]
    groups = out.shape[3] // group
    scale = 1.0 / (SPECTRA * own.shape[0] // CORES)
    mine = halves(own[...])
    wide = mine.astype(jnp.float32).reshape(-1, 2, SPECTRA, group)
    turned = jnp.stack([-wide[:, 1], wide[:, 0]], 1).reshape(mine.shape)
    lhs = jnp.concatenate([wide.reshape(mine.shape), turned], 1)
    lhs = jnp.transpose(lhs).astype(jnp.bfloat16)
    far = jnp.concatenate([far_low[...], far_high[...]], 0)
    sources = [(0, mine), (groups - 1, halves(left[...])), (1, halves(right[...])), (2, halves(far))]
    for ahead, columns in sources:
        product = lax.dot_general(
            lhs, columns, (((1,), (0,)), ((), ())), preferred_element_type=jnp.float32
        )
        product = (product * scale).astype(jnp.bfloat16)
        at = pl.ds(pl.multiple_of(lax.rem(me + ahead, groups) * group, group), group)
        for z in range(2):
            out[0, z, :, at] = product[z * group : (z + 1) * group]


def correlate(place, parts, first, shape, result):
    own = parts[0]
    slots = own.shape[1]

    def part_spec(part):
        return pl.BlockSpec((part.shape[0], 1) + part.shape[2:], lambda j: (0, j, 0, 0))

    in_specs = [pl.BlockSpec(memory_space=pltpu.SMEM)] + [part_spec(part) for part in parts]
    operands = (place,) + tuple(parts)
    aliases = {}
    if result is not None:
        in_specs.append(pl.BlockSpec(memory_space=pl.ANY))
        aliases = {len(operands): 0}
        operands = operands + (result,)
    return pl.pallas_call(
        correlate_kernel,
        grid=(slots,),
        out_shape=jax.ShapeDtypeStruct(shape, jnp.bfloat16),
        in_specs=in_specs,
        out_specs=pl.BlockSpec((1,) + shape[1:], lambda j: (first + j, 0, 0, 0)),
        input_output_aliases=aliases,
        compiler_params=pltpu.CompilerParams(
            dimension_semantics=("arbitrary",), vmem_limit_bytes=VMEM
        ),
        name="correlate",
    )(*operands)


def body(voltage, flags, owner_slot):
    owners = lax.axis_size("freq")
    groups = lax.axis_size("feed")
    chips = owners // CORES
    band = owner_slot.shape[0]
    feeds = voltage.shape[1]
    half = feeds // CORES
    position = lax.axis_index("freq")
    core = position % CORES
    me = lax.axis_index("feed")
    place = jnp.stack([core, (position >= CORES).astype(jnp.int32), me]).astype(jnp.int32)

    after = [
        moved(
            voltage[:, c * half : (c + 1) * half, : 2 * CH],
            "freq",
            [(CORES * (k + 1), CORES * k + c) for k in range(chips - 1)],
        )
        for c in range(CORES)
    ]
    other = moved(
        lax.dynamic_slice_in_dim(voltage, (1 - core) * half, half, 1),
        "freq",
        [(k, k ^ 1) for k in range(owners)],
    )
    before = [
        moved(
            voltage[:, c * half : (c + 1) * half, (BLOCKS - 1) * CH :],
            "freq",
            [(CORES * k + CORES - 1, CORES * ((k + 1) % chips) + c) for k in range(chips)],
        )
        for c in range(CORES)
    ]
    table = jnp.asarray(tables(band))
    kept = flags[0].astype(jnp.float32) * (1.0 / math.sqrt(CH))
    chosen = []
    first = 0
    for slots in CHUNKS:
        row = jnp.arange(owners * slots, dtype=jnp.int32)
        slot = row // slots * CAP + first + row % slots
        select = jnp.where(owner_slot[None, :] == slot[:, None], kept[None, :], 0.0)
        chosen.append(
            jnp.dot(
                select.astype(jnp.bfloat16), table, preferred_element_type=jnp.float32
            ).astype(jnp.bfloat16)
        )
        first += slots

    low = core == 0
    weighted = weigh(
        place,
        voltage,
        other,
        jnp.where(low, after[0], after[1]),
        jnp.where(low, before[0], before[1]),
    )
    ring_up = [(k, (k + 1) % groups) for k in range(groups)]
    ring_down = [(k, (k - 1) % groups) for k in range(groups)]
    shape = (CAP, 2, feeds, feeds * groups)
    result = None
    first = 0
    for index, slots in enumerate(CHUNKS):
        spectra = transform(chosen[index], weighted)
        own = lax.all_to_all(
            spectra.reshape(owners, slots, 2 * SPECTRA, half), "freq", 0, 0, tiled=True
        )
        left = moved(own, "feed", ring_up)
        right = moved(own, "feed", ring_down)
        far_low = moved(left[: owners // 2], "feed", ring_up)
        far_high = moved(right[owners // 2 :], "feed", ring_down)
        result = correlate(place, (own, left, right, far_low, far_high), first, shape, result)
        first += slots
    return result


def solution(mesh):
    placed = (P(None, "feed", "freq"), P("feed", None), P())
    return jax.shard_map(
        body, mesh=mesh, in_specs=placed, out_specs=P("freq", None, "feed", None), check_vma=False
    )
```

```python
import math

import jax
import jax.numpy as jnp
import ml_dtypes
import numpy as np
from jax import lax
from jax.experimental import pallas as pl
from jax.experimental.pallas import tpu as pltpu
from jax.sharding import PartitionSpec as P

CH = 1024
TAPS = 4
BAND_LO = 256
CAP = 20
CORES = 2
BLOCKS = 4
PIECES = (8, 12)
EARLY = ((0, 4),)
LATE = ((0, 1), (4, 3))
STEP = 2
AHEAD = (0, 3, 1, 2)
VMEM = 60 * 1024 * 1024
WEIGHT = pl.CostEstimate(flops=10**13, bytes_accessed=2 * 10**10, transcendentals=0)


def prototype():
    total = TAPS * CH
    position = np.arange(total).astype(np.float32)
    offset = (position - total / 2 + 0.5) / CH
    taper = 0.5 - 0.5 * np.cos(2 * np.pi * (position + 0.5) / total)
    coeffs = np.sinc(offset) * taper
    coeffs = coeffs * np.sqrt(CH / np.sum(coeffs * coeffs))
    return coeffs.reshape(TAPS, CH).astype(np.float32)


def tables(band):
    sample = np.arange(CH)
    channel = np.arange(band) + BAND_LO
    phase = (channel[:, None] * sample[None, :] % CH).astype(np.float32) * np.float32(2 * np.pi / CH)
    cosine = np.cos(phase).astype(ml_dtypes.bfloat16)
    sine = np.sin(phase).astype(ml_dtypes.bfloat16)
    return np.concatenate([cosine, sine], 1)


def after(value, *earlier):
    return lax.optimization_barrier((value,) + earlier)[0]


def pick_kernel(place, voltage, *rest):
    outs, sems = rest[:-1], rest[-1]
    core = place[0]
    half = voltage.shape[1] // CORES
    copies = []
    for k, out in enumerate(outs):
        width = out.shape[2]
        first = core * width if width < voltage.shape[2] else 0
        base = (1 - core if k + 1 == len(outs) else core) * half
        source = voltage.at[
            :, pl.ds(pl.multiple_of(base, half), half), pl.ds(pl.multiple_of(first, CH), width)
        ]
        copies.append(pltpu.make_async_copy(source, out, sems.at[k]))
    for copy in copies:
        copy.start()
    for copy in copies:
        copy.wait()


def pick(place, voltage, count, width):
    half = voltage.shape[1] // CORES
    return pl.pallas_call(
        pick_kernel,
        out_shape=[jax.ShapeDtypeStruct((2, half, width), jnp.bfloat16)] * count,
        in_specs=[pl.BlockSpec(memory_space=pltpu.SMEM), pl.BlockSpec(memory_space=pl.ANY)],
        out_specs=[pl.BlockSpec(memory_space=pltpu.VMEM)] * count,
        scratch_shapes=[pltpu.SemaphoreType.DMA((count,))],
        compiler_params=pltpu.CompilerParams(vmem_limit_bytes=VMEM),
        cost_estimate=WEIGHT,
        name="pick",
    )(place, voltage)


def channelize_kernel(windows, pieces, place, voltage, other, *rest):
    second = len(windows) == 2
    halo = rest[: 2 * second]
    rest = rest[2 * second :]
    coeffs, table = rest[:2]
    outs = rest[2:-5]
    held, weighted, chosen, spread, sems = rest[-5:]
    core = place[0]
    half = voltage.shape[1] // CORES
    own_rows = pl.ds(pl.multiple_of(core * half, half), half)
    tail = TAPS - 1
    fetch = pltpu.make_async_copy(table, chosen, sems.at[4])
    fetch.start()

    def load(parts):
        copies = []
        for source, first, count, at in parts:
            if source is voltage:
                block = voltage.at[:, own_rows, pl.ds(first * CH, count * CH)]
            else:
                block = source.at[:, :, pl.ds(first * CH, count * CH)]
            target = held.at[:, :, pl.ds(at * CH, count * CH)]
            copies.append(pltpu.make_async_copy(block, target, sems.at[len(copies)]))
        for copy in copies:
            copy.start()
        for copy in copies:
            copy.wait()

    def load_for(low, high, nearer):
        if second:
            previous, following = nearer
            load(
                [
                    (previous, 1, 1, 0),
                    (low, 0, tail, 1),
                    (high, 0, BLOCKS, BLOCKS),
                    (following, 0, 2, 2 * BLOCKS),
                ]
            )
        else:
            load([(low, 0, BLOCKS, 0), (high, 0, tail, BLOCKS)])

    @pl.when(core == 0)
    def _():
        load_for(voltage, other, halo[::-1])

    @pl.when(core != 0)
    def _():
        load_for(other, voltage, halo)

    keep = place[2].astype(jnp.float32)
    rows = 16
    width = 256

    def step(index, carry):
        at = pl.ds(pl.multiple_of(index * rows, rows), rows)
        for z in range(2):
            for start in range(0, CH, width):
                taps = [coeffs[p : p + 1, pl.ds(start, width)] for p in range(TAPS)]
                s = 0
                for window, (base, count) in enumerate(windows):
                    blocks = [
                        held[z, at, pl.ds((base + b) * CH + start, width)].astype(jnp.float32)
                        for b in range(count + TAPS - 1)
                    ]
                    for k in range(count):
                        total = blocks[k] * taps[0]
                        for p in range(1, TAPS):
                            tap = taps[p] * keep if second and window == 0 else taps[p]
                            total = total + blocks[k + p] * tap
                        weighted[z, s, at, pl.ds(start, width)] = total.astype(jnp.bfloat16)
                        s += 1
        return carry

    lax.fori_loop(0, half // rows, step, 0)
    fetch.wait()
    owners = outs[0].shape[0]
    places = [(out, j) for out in outs for j in range(out.shape[1])]
    columns = BLOCKS * half
    samples = weighted[...].reshape(2 * columns, CH)
    base = 0
    for slots in pieces:
        number = owners * slots
        at = pl.ds(base, number)
        out, first = places[base // owners]
        both = jnp.concatenate([chosen[at, :CH], chosen[at, CH:]], 0)
        product = lax.dot_general(
            both, samples, (((1,), (1,)), ((), ())), preferred_element_type=jnp.float32
        )
        parts = (
            product[:number, :columns] + product[number:, columns:],
            product[:number, columns:] - product[number:, :columns],
        )
        for z in range(2):
            for s in range(BLOCKS):
                spread[pl.ds(z * BLOCKS + s, number, stride=2 * BLOCKS), :] = parts[z][
                    :, s * half : (s + 1) * half
                ]
        out[:, first : first + slots] = (
            spread[pl.ds(0, number * 2 * BLOCKS), :]
            .reshape(owners, slots, 2 * BLOCKS, half)
            .astype(jnp.bfloat16)
        )
        base += number


def channelize(place, voltage, other, halo, table, windows, pieces, sent, owners):
    half = voltage.shape[1] // CORES
    operands = (voltage, other) + halo
    span = sum(count + TAPS - 1 for _, count in windows)
    anywhere = pl.BlockSpec(memory_space=pl.ANY)
    vmem = pl.BlockSpec(memory_space=pltpu.VMEM)

    def kernel(*refs):
        channelize_kernel(windows, pieces, *refs)

    return pl.pallas_call(
        kernel,
        out_shape=[
            jax.ShapeDtypeStruct((owners, slots, 2 * BLOCKS, half), jnp.bfloat16)
            for slots in sent
        ],
        in_specs=[pl.BlockSpec(memory_space=pltpu.SMEM)]
        + [anywhere] * len(operands)
        + [vmem, anywhere],
        out_specs=[vmem] * len(sent),
        scratch_shapes=[
            pltpu.VMEM((2, half, span * CH), jnp.bfloat16),
            pltpu.VMEM((2, BLOCKS, half, CH), jnp.bfloat16),
            pltpu.VMEM(table.shape, jnp.bfloat16),
            pltpu.VMEM((owners * max(pieces) * 2 * BLOCKS, half), jnp.float32),
            pltpu.SemaphoreType.DMA((5,)),
        ],
        compiler_params=pltpu.CompilerParams(vmem_limit_bytes=VMEM),
        cost_estimate=WEIGHT,
        name="channelize",
    )(place, *operands, jnp.asarray(prototype()), table)


def gathered(part, j):
    count, _, rows, lanes = part.shape
    wide = part[:, j].astype(jnp.float32).reshape(count // CORES, CORES, rows, lanes)
    return jnp.concatenate([wide[:, core] for core in range(CORES)], 2)


def correlate_kernel(parts_of, place, *refs):
    out = refs[-1]
    me = place[1]
    group = out.shape[2]
    groups = out.shape[3] // group
    sources = []
    at = 0
    for count in parts_of:
        sources.append(refs[at : at + count])
        at += count
    scale = CORES / (2 * BLOCKS * refs[0].shape[0])
    row = lax.broadcasted_iota(jnp.int32, (1, 2 * BLOCKS, group), 1)
    sign = jnp.where(row < BLOCKS, -1.0, 1.0)
    for j in range(out.shape[0]):
        for ahead, source in zip(AHEAD, sources):
            wide = jnp.concatenate([gathered(piece, j) for piece in source], 0)
            if ahead == 0:
                mine = wide * scale
                turned = pltpu.roll(mine, BLOCKS, 1) * sign
                lhs = jnp.concatenate([mine, turned], 2)
                lhs = lhs.reshape(-1, 2 * group).astype(jnp.bfloat16)
                lhs = jnp.transpose(lhs)
            product = lax.dot_general(
                lhs,
                wide.reshape(-1, group).astype(jnp.bfloat16),
                (((1,), (0,)), ((), ())),
                preferred_element_type=jnp.float32,
            ).astype(jnp.bfloat16)
            at = pl.ds(pl.multiple_of(lax.rem(me + ahead, groups) * group, group), group)
            for z in range(2):
                out[j, z, :, at] = product[z * group : (z + 1) * group]


def correlate(place, sources, first, slots, shape, result):
    in_specs = []
    operands = []
    for ahead, source in zip(AHEAD, sources):
        for part, starts, axis in source:
            skip = (first - starts) // STEP
            if axis is None:
                block = (part.shape[0], STEP) + part.shape[2:]
            else:
                block = [None if k == axis else part.shape[k] for k in range(part.ndim)]
                block[2] = STEP
            groups = None if axis is None else part.shape[axis]

            def index(j, place, ahead=ahead, skip=skip, axis=axis, groups=groups):
                if axis is None:
                    return 0, skip + j, 0, 0
                which = lax.rem(place[1] + ahead, groups)
                return (which, 0, skip + j, 0, 0) if axis == 0 else (0, which, skip + j, 0, 0)

            in_specs.append(pl.BlockSpec(tuple(block), index))
            operands.append(part)
    parts_of = tuple(len(source) for source in sources)
    aliases = {}
    if result is not None:
        in_specs.append(pl.BlockSpec(memory_space=pl.ANY))
        aliases = {len(operands) + 1: 0}
        operands.append(result)

    def kernel(*refs):
        correlate_kernel(parts_of, *refs)

    return pl.pallas_call(
        kernel,
        out_shape=jax.ShapeDtypeStruct(shape, jnp.bfloat16),
        grid_spec=pltpu.PrefetchScalarGridSpec(
            num_scalar_prefetch=1,
            grid=(slots // STEP,),
            in_specs=in_specs,
            out_specs=pl.BlockSpec(
                (STEP,) + shape[1:], lambda j, place: (first // STEP + j, 0, 0, 0)
            ),
        ),
        input_output_aliases=aliases,
        compiler_params=pltpu.CompilerParams(
            dimension_semantics=("arbitrary",), vmem_limit_bytes=VMEM
        ),
        cost_estimate=WEIGHT,
        name="correlate",
    )(place, *operands)


def body(voltage, flags, owner_slot):
    owners = lax.axis_size("freq")
    groups = lax.axis_size("feed")
    chips = owners // CORES
    band = owner_slot.shape[0]
    feeds = voltage.shape[1]
    position = lax.axis_index("freq")
    place = jnp.stack(
        [position % CORES, lax.axis_index("feed"), (position >= CORES).astype(jnp.int32)]
    ).astype(jnp.int32)

    (given,) = pick(place, voltage, 1, voltage.shape[2])
    other = lax.ppermute(given, "freq", [(k, k ^ 1) for k in range(owners)])
    edges = pick(place, after(voltage, given), 2, 2 * CH)
    halo = []
    for k, edge in enumerate(edges):
        down = [(CORES * (c + 1), CORES * c + k) for c in range(chips - 1)]
        up = [(CORES * c + 1, CORES * ((c + 1) % chips) + 1 - k) for c in range(chips)]
        halo.append(lax.ppermute(edge, "freq", down + up))
    kept = flags[0].astype(jnp.float32) * (1.0 / math.sqrt(CH))
    slot = []
    first = 0
    for slots in PIECES:
        row = np.arange(owners * slots)
        slot.append(row // slots * CAP + first + row % slots)
        first += slots
    slot = jnp.asarray(np.concatenate(slot), jnp.int32)
    select = jnp.where(owner_slot[None, :] == slot[:, None], kept[None, :], 0.0)
    table = jnp.dot(
        select.astype(jnp.bfloat16), jnp.asarray(tables(band)), preferred_element_type=jnp.float32
    ).astype(jnp.bfloat16)

    def ring(value, steps):
        return lax.ppermute(value, "feed", [(k, (k + steps) % groups) for k in range(groups)])

    def exchanged(spectra):
        return lax.all_to_all(spectra, "freq", 0, 0, tiled=True)

    def far(left, right):
        middle = owners // 2
        return ring(left[:middle], 1), ring(right[middle:], -1)

    small, large = PIECES
    a0, a1 = channelize(place, after(voltage, *edges), other, (), table, EARLY, PIECES, PIECES, owners)
    all_a0 = lax.all_gather(a0, "feed")
    own_a1 = exchanged(a1)
    b0, b1 = channelize(place, voltage, other, tuple(halo), table, LATE, PIECES, PIECES, owners)
    b0, b1 = channelize(place, voltage, other, tuple(halo), table, LATE, PIECES, PIECES, owners)
    own_a1 = after(own_a1, b1)
    left_a1, right_a1 = ring(own_a1, 1), ring(own_a1, -1)
    far_a1 = far(left_a1, right_a1)
    own_b1 = exchanged(after(b1, own_a1, all_a0))
    own_b0 = exchanged(after(b0, own_b1, *far_a1))
    left_b1, right_b1 = ring(own_b1, 1), ring(own_b1, -1)
    left_b0, right_b0 = ring(own_b0, 1), ring(own_b0, -1)
    all_a0 = exchanged(after(jnp.swapaxes(all_a0, 0, 1), left_b1, right_b1))
    far_b1 = far(left_b1, right_b1)
    far_b0 = far(left_b0, right_b0)

    shape = (CAP, 2, feeds, feeds * groups)

    def whole(parts, first):
        return [
            [(part, first, None) for part in (group if isinstance(group, tuple) else (group,))]
            for group in parts
        ]

    early = whole((own_a1, left_a1, right_a1, far_a1), small)
    late = whole((own_b1, left_b1, right_b1, far_b1), small)
    sources = [one + two for one, two in zip(early, late)]
    result = correlate(place, sources, small, large, shape, None)
    late = whole((own_b0, left_b0, right_b0, far_b0), 0)
    sources = [[(all_a0, 0, 1)] + two for two in late]
    return correlate(place, sources, 0, small, shape, result)


def solution(mesh):
    placed = (P(None, "feed", "freq"), P("feed", None), P())
    return jax.shard_map(
        body, mesh=mesh, in_specs=placed, out_specs=P("freq", None, "feed", None), check_vma=False
    )
```

```python
import math

import jax
import jax.numpy as jnp
import ml_dtypes
import numpy as np
from jax import lax
from jax.experimental import pallas as pl
from jax.experimental.pallas import tpu as pltpu
from jax.sharding import PartitionSpec as P

CH = 1024
TAPS = 4
BAND_LO = 256
CAP = 20
CORES = 2
BLOCKS = 4
PIECES = (8, 12)
EARLY = ((0, 4),)
LATE = ((0, 1), (4, 3))
STEP = 4
AHEAD = (0, 3, 1, 2)
VMEM = 60 * 1024 * 1024
WEIGHT = pl.CostEstimate(flops=10**13, bytes_accessed=2 * 10**10, transcendentals=0)


def prototype():
    total = TAPS * CH
    position = np.arange(total).astype(np.float32)
    offset = (position - total / 2 + 0.5) / CH
    taper = 0.5 - 0.5 * np.cos(2 * np.pi * (position + 0.5) / total)
    coeffs = np.sinc(offset) * taper
    coeffs = coeffs * np.sqrt(CH / np.sum(coeffs * coeffs))
    return coeffs.reshape(TAPS, CH).astype(np.float32)


def tables(band):
    sample = np.arange(CH)
    channel = np.arange(band) + BAND_LO
    phase = (channel[:, None] * sample[None, :] % CH).astype(np.float32) * np.float32(2 * np.pi / CH)
    cosine = np.cos(phase).astype(ml_dtypes.bfloat16)
    sine = np.sin(phase).astype(ml_dtypes.bfloat16)
    return np.concatenate([cosine, sine], 1)


def after(value, *earlier):
    return lax.optimization_barrier((value,) + earlier)[0]


def after_all(values, earlier):
    return lax.optimization_barrier(tuple(values) + tuple(earlier))[: len(values)]


def pick_kernel(place, voltage, *rest):
    outs, sems = rest[:-1], rest[-1]
    core = place[0]
    half = voltage.shape[1] // CORES
    copies = []
    for k, out in enumerate(outs):
        width = out.shape[2]
        first = core * width if width < voltage.shape[2] else 0
        base = (1 - core if k + 1 == len(outs) else core) * half
        source = voltage.at[
            :, pl.ds(pl.multiple_of(base, half), half), pl.ds(pl.multiple_of(first, CH), width)
        ]
        copies.append(pltpu.make_async_copy(source, out, sems.at[k]))
    for copy in copies:
        copy.start()
    for copy in copies:
        copy.wait()


def pick(place, voltage, count, width):
    half = voltage.shape[1] // CORES
    return pl.pallas_call(
        pick_kernel,
        out_shape=[jax.ShapeDtypeStruct((2, half, width), jnp.bfloat16)] * count,
        in_specs=[pl.BlockSpec(memory_space=pltpu.SMEM), pl.BlockSpec(memory_space=pl.ANY)],
        out_specs=[pl.BlockSpec(memory_space=pltpu.VMEM)] * count,
        scratch_shapes=[pltpu.SemaphoreType.DMA((count,))],
        compiler_params=pltpu.CompilerParams(vmem_limit_bytes=VMEM),
        cost_estimate=WEIGHT,
        name="pick",
    )(place, voltage)


def channelize_kernel(windows, pieces, place, voltage, other, *rest):
    second = len(windows) == 2
    halo = rest[: 2 * second]
    rest = rest[2 * second :]
    coeffs, table = rest[:2]
    outs = rest[2:-5]
    held, weighted, chosen, spread, sems = rest[-5:]
    core = place[0]
    half = voltage.shape[1] // CORES
    own_rows = pl.ds(pl.multiple_of(core * half, half), half)
    tail = TAPS - 1
    fetch = pltpu.make_async_copy(table, chosen, sems.at[4])
    fetch.start()

    def load(parts):
        copies = []
        for source, first, count, at in parts:
            if source is voltage:
                block = voltage.at[:, own_rows, pl.ds(first * CH, count * CH)]
            else:
                block = source.at[:, :, pl.ds(first * CH, count * CH)]
            target = held.at[:, :, pl.ds(at * CH, count * CH)]
            copies.append(pltpu.make_async_copy(block, target, sems.at[len(copies)]))
        for copy in copies:
            copy.start()
        for copy in copies:
            copy.wait()

    def load_for(low, high, nearer):
        if second:
            previous, following = nearer
            load(
                [
                    (previous, 1, 1, 0),
                    (low, 0, tail, 1),
                    (high, 0, BLOCKS, BLOCKS),
                    (following, 0, 2, 2 * BLOCKS),
                ]
            )
        else:
            load([(low, 0, BLOCKS, 0), (high, 0, tail, BLOCKS)])

    @pl.when(core == 0)
    def _():
        load_for(voltage, other, halo[::-1])

    @pl.when(core != 0)
    def _():
        load_for(other, voltage, halo)

    keep = place[2].astype(jnp.float32)
    rows = 16
    width = 256

    def step(index, carry):
        at = pl.ds(pl.multiple_of(index * rows, rows), rows)
        for z in range(2):
            for start in range(0, CH, width):
                taps = [coeffs[p : p + 1, pl.ds(start, width)] for p in range(TAPS)]
                s = 0
                for window, (base, count) in enumerate(windows):
                    blocks = [
                        held[z, at, pl.ds((base + b) * CH + start, width)].astype(jnp.float32)
                        for b in range(count + TAPS - 1)
                    ]
                    for k in range(count):
                        total = blocks[k] * taps[0]
                        for p in range(1, TAPS):
                            tap = taps[p] * keep if second and window == 0 else taps[p]
                            total = total + blocks[k + p] * tap
                        weighted[z, s, at, pl.ds(start, width)] = total.astype(jnp.bfloat16)
                        s += 1
        return carry

    lax.fori_loop(0, half // rows, step, 0)
    fetch.wait()
    owners = outs[0].shape[0]
    places = [(out, j) for out in outs for j in range(out.shape[1])]
    columns = BLOCKS * half
    samples = weighted[...].reshape(2 * columns, CH)
    base = 0
    for slots in pieces:
        number = owners * slots
        at = pl.ds(base, number)
        out, first = places[base // owners]
        both = jnp.concatenate([chosen[at, :CH], chosen[at, CH:]], 0)
        product = lax.dot_general(
            both, samples, (((1,), (1,)), ((), ())), preferred_element_type=jnp.float32
        )
        parts = (
            product[:number, :columns] + product[number:, columns:],
            product[:number, columns:] - product[number:, :columns],
        )
        for z in range(2):
            for s in range(BLOCKS):
                spread[pl.ds(z * BLOCKS + s, number, stride=2 * BLOCKS), :] = parts[z][
                    :, s * half : (s + 1) * half
                ]
        out[:, first : first + slots] = (
            spread[pl.ds(0, number * 2 * BLOCKS), :]
            .reshape(owners, slots, 2 * BLOCKS, half)
            .astype(jnp.bfloat16)
        )
        base += number


def channelize(place, voltage, other, halo, table, windows, pieces, sent, owners):
    half = voltage.shape[1] // CORES
    operands = (voltage, other) + halo
    span = sum(count + TAPS - 1 for _, count in windows)
    anywhere = pl.BlockSpec(memory_space=pl.ANY)
    vmem = pl.BlockSpec(memory_space=pltpu.VMEM)

    def kernel(*refs):
        channelize_kernel(windows, pieces, *refs)

    return pl.pallas_call(
        kernel,
        out_shape=[
            jax.ShapeDtypeStruct((owners, slots, 2 * BLOCKS, half), jnp.bfloat16)
            for slots in sent
        ],
        in_specs=[pl.BlockSpec(memory_space=pltpu.SMEM)]
        + [anywhere] * len(operands)
        + [vmem, anywhere],
        out_specs=[vmem] * len(sent),
        scratch_shapes=[
            pltpu.VMEM((2, half, span * CH), jnp.bfloat16),
            pltpu.VMEM((2, BLOCKS, half, CH), jnp.bfloat16),
            pltpu.VMEM(table.shape, jnp.bfloat16),
            pltpu.VMEM((owners * max(pieces) * 2 * BLOCKS, half), jnp.float32),
            pltpu.SemaphoreType.DMA((5,)),
        ],
        compiler_params=pltpu.CompilerParams(vmem_limit_bytes=VMEM),
        cost_estimate=WEIGHT,
        name="channelize",
    )(place, *operands, jnp.asarray(prototype()), table)


def pack_kernel(*refs):
    out = refs[-1]
    slots = refs[0].shape[1]
    for k, ref in enumerate(refs[:4]):
        out[:, k * slots : (k + 1) * slots] = ref[...]


def pack(parts, wait):
    count, slots, rows, lanes = parts[0].shape
    step = count // 8
    block = pl.BlockSpec((step, slots, rows, lanes), lambda k: (k, 0, 0, 0))
    return pl.pallas_call(
        pack_kernel,
        grid=(count // step,),
        out_shape=jax.ShapeDtypeStruct((count, len(parts) * slots, rows, lanes), jnp.bfloat16),
        in_specs=[block] * len(parts),
        out_specs=pl.BlockSpec((step, len(parts) * slots, rows, lanes), lambda k: (k, 0, 0, 0)),
        compiler_params=pltpu.CompilerParams(
            dimension_semantics=("arbitrary",), vmem_limit_bytes=VMEM
        ),
        cost_estimate=WEIGHT,
        name="pack",
    )(*after_all(parts, wait))


def gathered(part, j):
    count, _, rows, lanes = part.shape
    wide = part[:, j].astype(jnp.float32).reshape(count // CORES, CORES, rows, lanes)
    return jnp.concatenate([wide[:, core] for core in range(CORES)], 2)


def correlate_kernel(parts_of, place, *refs):
    out = refs[-1]
    me = place[1]
    group = out.shape[2]
    groups = out.shape[3] // group
    sources = []
    at = 0
    for count in parts_of:
        sources.append(refs[at : at + count])
        at += count
    scale = CORES / (2 * BLOCKS * refs[0].shape[0])
    row = lax.broadcasted_iota(jnp.int32, (1, 2 * BLOCKS, group), 1)
    sign = jnp.where(row < BLOCKS, -1.0, 1.0)
    for j in range(out.shape[0]):
        for ahead, source in zip(AHEAD, sources):
            wide = jnp.concatenate([gathered(piece, j) for piece in source], 0)
            if ahead == 0:
                mine = wide * scale
                turned = pltpu.roll(mine, BLOCKS, 1) * sign
                lhs = jnp.concatenate([mine, turned], 2)
                lhs = lhs.reshape(-1, 2 * group).astype(jnp.bfloat16)
                lhs = jnp.transpose(lhs)
            product = lax.dot_general(
                lhs,
                wide.reshape(-1, group).astype(jnp.bfloat16),
                (((1,), (0,)), ((), ())),
                preferred_element_type=jnp.float32,
            ).astype(jnp.bfloat16)
            at = pl.ds(pl.multiple_of(lax.rem(me + ahead, groups) * group, group), group)
            for z in range(2):
                out[j, z, :, at] = product[z * group : (z + 1) * group]


def correlate(place, sources, first, slots, shape, result):
    in_specs = []
    operands = []
    for ahead, source in zip(AHEAD, sources):
        for part, starts, axis in source:
            skip = (first - starts) // STEP
            if axis is None:
                block = (part.shape[0], STEP) + part.shape[2:]
            else:
                block = [None if k == axis else part.shape[k] for k in range(part.ndim)]
                block[2] = STEP
            groups = None if axis is None else part.shape[axis]

            def index(j, place, ahead=ahead, skip=skip, axis=axis, groups=groups):
                if axis is None:
                    return 0, skip + j, 0, 0
                which = lax.rem(place[1] + ahead, groups)
                return (which, 0, skip + j, 0, 0) if axis == 0 else (0, which, skip + j, 0, 0)

            in_specs.append(pl.BlockSpec(tuple(block), index))
            operands.append(part)
    parts_of = tuple(len(source) for source in sources)
    aliases = {}
    if result is not None:
        in_specs.append(pl.BlockSpec(memory_space=pl.ANY))
        aliases = {len(operands) + 1: 0}
        operands.append(result)

    def kernel(*refs):
        correlate_kernel(parts_of, *refs)

    return pl.pallas_call(
        kernel,
        out_shape=jax.ShapeDtypeStruct(shape, jnp.bfloat16),
        grid_spec=pltpu.PrefetchScalarGridSpec(
            num_scalar_prefetch=1,
            grid=(slots // STEP,),
            in_specs=in_specs,
            out_specs=pl.BlockSpec(
                (STEP,) + shape[1:], lambda j, place: (first // STEP + j, 0, 0, 0)
            ),
        ),
        input_output_aliases=aliases,
        compiler_params=pltpu.CompilerParams(
            dimension_semantics=("arbitrary",), vmem_limit_bytes=VMEM
        ),
        cost_estimate=pl.CostEstimate(flops=10**10, bytes_accessed=4 * 10**7, transcendentals=0),
        name="correlate",
    )(place, *operands)


def body(voltage, flags, owner_slot):
    owners = lax.axis_size("freq")
    groups = lax.axis_size("feed")
    chips = owners // CORES
    band = owner_slot.shape[0]
    feeds = voltage.shape[1]
    position = lax.axis_index("freq")
    place = jnp.stack(
        [position % CORES, lax.axis_index("feed"), (position >= CORES).astype(jnp.int32)]
    ).astype(jnp.int32)

    (given,) = pick(place, voltage, 1, voltage.shape[2])
    other = lax.ppermute(given, "freq", [(k, k ^ 1) for k in range(owners)])
    edges = pick(place, after(voltage, given), 2, 2 * CH)
    halo = []
    for k, edge in enumerate(edges):
        down = [(CORES * (c + 1), CORES * c + k) for c in range(chips - 1)]
        up = [(CORES * c + 1, CORES * ((c + 1) % chips) + 1 - k) for c in range(chips)]
        halo.append(lax.ppermute(edge, "freq", down + up))
    kept = flags[0].astype(jnp.float32) * (1.0 / math.sqrt(CH))
    slot = []
    first = 0
    for slots in PIECES:
        row = np.arange(owners * slots)
        slot.append(row // slots * CAP + first + row % slots)
        first += slots
    slot = jnp.asarray(np.concatenate(slot), jnp.int32)
    select = jnp.where(owner_slot[None, :] == slot[:, None], kept[None, :], 0.0)
    table = jnp.dot(
        select.astype(jnp.bfloat16), jnp.asarray(tables(band)), preferred_element_type=jnp.float32
    ).astype(jnp.bfloat16)

    def ring(value, steps):
        return lax.ppermute(value, "feed", [(k, (k + steps) % groups) for k in range(groups)])

    def exchanged(spectra):
        return lax.all_to_all(spectra, "freq", 0, 0, tiled=True)

    def far(left, right):
        middle = owners // 2
        return ring(left[:middle], 1), ring(right[middle:], -1)

    small, large = PIECES
    a0, a1 = channelize(place, after(voltage, *edges), other, (), table, EARLY, PIECES, PIECES, owners)
    left_a0, right_a0, far_a0 = ring(a0, 1), ring(a0, -1), ring(a0, 2)
    own_a1 = exchanged(a1)
    (b,) = channelize(place, voltage, other, tuple(halo), table, LATE, PIECES, (CAP,), owners)
    (b,) = channelize(place, voltage, other, tuple(halo), table, LATE, PIECES, (CAP,), owners)
    own_a1 = after(own_a1, b, left_a0, right_a0, far_a0)
    left_a1, right_a1 = ring(own_a1, 1), ring(own_a1, -1)
    far_a1 = far(left_a1, right_a1)
    own_b = exchanged(after(b, own_a1))
    all_a0 = pack((a0, left_a0, right_a0, far_a0), (left_a1, right_a1))
    own_b = after(own_b, all_a0)
    ready_b = after(own_b, *far_a1)
    own_b1 = ready_b[:, small:]
    own_b0 = ready_b[:, :small]
    left_b1, right_b1 = ring(own_b1, 1), ring(own_b1, -1)
    left_b0, right_b0 = ring(own_b0, 1), ring(own_b0, -1)
    all_a0 = exchanged(after(all_a0, ready_b))
    far_b1 = far(left_b1, right_b1)
    far_b0 = far(left_b0, right_b0)

    shape = (CAP, 2, feeds, feeds * groups)

    def whole(own, parts, first):
        return [[own]] + [
            [(part, first, None) for part in (group if isinstance(group, tuple) else (group,))]
            for group in parts
        ]

    early = whole((own_a1, small, None), (left_a1, right_a1, far_a1), small)
    late = whole((own_b, 0, None), (left_b1, right_b1, far_b1), small)
    sources = [one + two for one, two in zip(early, late)]
    result = correlate(place, sources, small, large, shape, None)
    late = whole((own_b, 0, None), (left_b0, right_b0, far_b0), 0)
    sources = [[(all_a0, -small * k, None)] + two for k, two in enumerate(late)]
    return correlate(place, sources, 0, small, shape, result)


def solution(mesh):
    placed = (P(None, "feed", "freq"), P("feed", None), P())
    return jax.shard_map(
        body, mesh=mesh, in_specs=placed, out_specs=P("freq", None, "feed", None), check_vma=False
    )
```

```python
import math

import jax
import jax.numpy as jnp
import ml_dtypes
import numpy as np
from jax import lax
from jax.experimental import pallas as pl
from jax.experimental.pallas import tpu as pltpu
from jax.sharding import PartitionSpec as P

CH = 1024
TAPS = 4
BAND_LO = 256
CAP = 20
CORES = 2
BLOCKS = 4
PIECES = (8, 12)
EARLY = ((0, 4),)
LATE = ((0, 1), (4, 3))
STEP = 4
AHEAD = (0, 3, 1, 2)
VMEM = 60 * 1024 * 1024
WEIGHT = pl.CostEstimate(flops=10**13, bytes_accessed=2 * 10**10, transcendentals=0)


def prototype():
    total = TAPS * CH
    position = np.arange(total).astype(np.float32)
    offset = (position - total / 2 + 0.5) / CH
    taper = 0.5 - 0.5 * np.cos(2 * np.pi * (position + 0.5) / total)
    coeffs = np.sinc(offset) * taper
    coeffs = coeffs * np.sqrt(CH / np.sum(coeffs * coeffs))
    return coeffs.reshape(TAPS, CH).astype(np.float32)


def tables(band):
    sample = np.arange(CH)
    channel = np.arange(band) + BAND_LO
    phase = (channel[:, None] * sample[None, :] % CH).astype(np.float32) * np.float32(2 * np.pi / CH)
    cosine = np.cos(phase).astype(ml_dtypes.bfloat16)
    sine = np.sin(phase).astype(ml_dtypes.bfloat16)
    return np.concatenate([cosine, sine], 1)


def after(value, *earlier):
    return lax.optimization_barrier((value,) + earlier)[0]


def after_all(values, earlier):
    return lax.optimization_barrier(tuple(values) + tuple(earlier))[: len(values)]


def pick_kernel(place, voltage, *rest):
    outs, sems = rest[:-1], rest[-1]
    core = place[0]
    half = voltage.shape[1] // CORES
    copies = []
    for k, out in enumerate(outs):
        width = out.shape[2]
        first = core * width if width < voltage.shape[2] else 0
        base = (1 - core if k + 1 == len(outs) else core) * half
        source = voltage.at[
            :, pl.ds(pl.multiple_of(base, half), half), pl.ds(pl.multiple_of(first, CH), width)
        ]
        copies.append(pltpu.make_async_copy(source, out, sems.at[k]))
    for copy in copies:
        copy.start()
    for copy in copies:
        copy.wait()


def pick(place, voltage, count, width):
    half = voltage.shape[1] // CORES
    return pl.pallas_call(
        pick_kernel,
        out_shape=[jax.ShapeDtypeStruct((2, half, width), jnp.bfloat16)] * count,
        in_specs=[pl.BlockSpec(memory_space=pltpu.SMEM), pl.BlockSpec(memory_space=pl.ANY)],
        out_specs=[pl.BlockSpec(memory_space=pltpu.VMEM)] * count,
        scratch_shapes=[pltpu.SemaphoreType.DMA((count,))],
        compiler_params=pltpu.CompilerParams(vmem_limit_bytes=VMEM),
        cost_estimate=WEIGHT,
        name="pick",
    )(place, voltage)


def channelize_kernel(windows, pieces, place, voltage, other, *rest):
    second = len(windows) == 2
    halo = rest[: 2 * second]
    rest = rest[2 * second :]
    coeffs, table = rest[:2]
    outs = rest[2:-5]
    held, weighted, chosen, spread, sems = rest[-5:]
    core = place[0]
    half = voltage.shape[1] // CORES
    own_rows = pl.ds(pl.multiple_of(core * half, half), half)
    tail = TAPS - 1
    fetch = pltpu.make_async_copy(table, chosen, sems.at[4])
    fetch.start()

    def load(parts):
        copies = []
        for source, first, count, at in parts:
            if source is voltage:
                block = voltage.at[:, own_rows, pl.ds(first * CH, count * CH)]
            else:
                block = source.at[:, :, pl.ds(first * CH, count * CH)]
            target = held.at[:, :, pl.ds(at * CH, count * CH)]
            copies.append(pltpu.make_async_copy(block, target, sems.at[len(copies)]))
        for copy in copies:
            copy.start()
        for copy in copies:
            copy.wait()

    def load_for(low, high, nearer):
        if second:
            previous, following = nearer
            load(
                [
                    (previous, 1, 1, 0),
                    (low, 0, tail, 1),
                    (high, 0, BLOCKS, BLOCKS),
                    (following, 0, 2, 2 * BLOCKS),
                ]
            )
        else:
            load([(low, 0, BLOCKS, 0), (high, 0, tail, BLOCKS)])

    @pl.when(core == 0)
    def _():
        load_for(voltage, other, halo[::-1])

    @pl.when(core != 0)
    def _():
        load_for(other, voltage, halo)

    keep = place[2].astype(jnp.float32)
    rows = 16
    width = 256

    def step(index, carry):
        at = pl.ds(pl.multiple_of(index * rows, rows), rows)
        for z in range(2):
            for start in range(0, CH, width):
                taps = [coeffs[p : p + 1, pl.ds(start, width)] for p in range(TAPS)]
                s = 0
                for window, (base, count) in enumerate(windows):
                    blocks = [
                        held[z, at, pl.ds((base + b) * CH + start, width)].astype(jnp.float32)
                        for b in range(count + TAPS - 1)
                    ]
                    for k in range(count):
                        total = blocks[k] * taps[0]
                        for p in range(1, TAPS):
                            tap = taps[p] * keep if second and window == 0 else taps[p]
                            total = total + blocks[k + p] * tap
                        weighted[z, s, at, pl.ds(start, width)] = total.astype(jnp.bfloat16)
                        s += 1
        return carry

    lax.fori_loop(0, half // rows, step, 0)
    fetch.wait()
    owners = outs[0].shape[0]
    places = [(out, j) for out in outs for j in range(out.shape[1])]
    columns = BLOCKS * half
    samples = weighted[...].reshape(2 * columns, CH)
    base = 0
    for slots in pieces:
        number = owners * slots
        at = pl.ds(base, number)
        out, first = places[base // owners]
        both = jnp.concatenate([chosen[at, :CH], chosen[at, CH:]], 0)
        product = lax.dot_general(
            both, samples, (((1,), (1,)), ((), ())), preferred_element_type=jnp.float32
        )
        parts = (
            product[:number, :columns] + product[number:, columns:],
            product[:number, columns:] - product[number:, :columns],
        )
        for z in range(2):
            for s in range(BLOCKS):
                spread[pl.ds(z * BLOCKS + s, number, stride=2 * BLOCKS), :] = parts[z][
                    :, s * half : (s + 1) * half
                ]
        out[:, first : first + slots] = (
            spread[pl.ds(0, number * 2 * BLOCKS), :]
            .reshape(owners, slots, 2 * BLOCKS, half)
            .astype(jnp.bfloat16)
        )
        base += number


def channelize(place, voltage, other, halo, table, windows, pieces, sent, owners):
    half = voltage.shape[1] // CORES
    operands = (voltage, other) + halo
    span = sum(count + TAPS - 1 for _, count in windows)
    anywhere = pl.BlockSpec(memory_space=pl.ANY)
    vmem = pl.BlockSpec(memory_space=pltpu.VMEM)

    def kernel(*refs):
        channelize_kernel(windows, pieces, *refs)

    return pl.pallas_call(
        kernel,
        out_shape=[
            jax.ShapeDtypeStruct((owners, slots, 2 * BLOCKS, half), jnp.bfloat16)
            for slots in sent
        ],
        in_specs=[pl.BlockSpec(memory_space=pltpu.SMEM)]
        + [anywhere] * len(operands)
        + [vmem, anywhere],
        out_specs=[vmem] * len(sent),
        scratch_shapes=[
            pltpu.VMEM((2, half, span * CH), jnp.bfloat16),
            pltpu.VMEM((2, BLOCKS, half, CH), jnp.bfloat16),
            pltpu.VMEM(table.shape, jnp.bfloat16),
            pltpu.VMEM((owners * max(pieces) * 2 * BLOCKS, half), jnp.float32),
            pltpu.SemaphoreType.DMA((5,)),
        ],
        compiler_params=pltpu.CompilerParams(vmem_limit_bytes=VMEM),
        cost_estimate=WEIGHT,
        name="channelize",
    )(place, *operands, jnp.asarray(prototype()), table)


def pack_kernel(*refs):
    out = refs[-1]
    slots = refs[0].shape[1]
    for k, ref in enumerate(refs[:4]):
        out[:, k * slots : (k + 1) * slots] = ref[...]


def pack(parts, wait):
    count, slots, rows, lanes = parts[0].shape
    step = count // 8
    block = pl.BlockSpec((step, slots, rows, lanes), lambda k: (k, 0, 0, 0))
    return pl.pallas_call(
        pack_kernel,
        grid=(count // step,),
        out_shape=jax.ShapeDtypeStruct((count, len(parts) * slots, rows, lanes), jnp.bfloat16),
        in_specs=[block] * len(parts),
        out_specs=pl.BlockSpec((step, len(parts) * slots, rows, lanes), lambda k: (k, 0, 0, 0)),
        compiler_params=pltpu.CompilerParams(
            dimension_semantics=("arbitrary",), vmem_limit_bytes=VMEM
        ),
        cost_estimate=WEIGHT,
        name="pack",
    )(*after_all(parts, wait))


def gathered(part, j):
    count, _, rows, lanes = part.shape
    wide = part[:, j].astype(jnp.float32).reshape(count // CORES, CORES, rows, lanes)
    return jnp.concatenate([wide[:, core] for core in range(CORES)], 2)


def left_operand(mine, scale):
    group = mine.shape[2]
    row = lax.broadcasted_iota(jnp.int32, (1, 2 * BLOCKS, group), 1)
    sign = jnp.where(row < BLOCKS, -1.0, 1.0)
    mine = mine * scale
    turned = pltpu.roll(mine, BLOCKS, 1) * sign
    both = jnp.concatenate([mine, turned], 2)
    return jnp.transpose(both.reshape(-1, 2 * group).astype(jnp.bfloat16))


def correlate_far_kernel(counts, place, *refs):
    out = refs[-1]
    group = out.shape[2]
    own, far = refs[: counts[0]], refs[counts[0] : sum(counts)]
    scale = CORES / (2 * BLOCKS * refs[0].shape[0])
    for j in range(out.shape[0]):
        mine = jnp.concatenate([gathered(piece, j) for piece in own], 0)
        wide = jnp.concatenate([gathered(piece, j) for piece in far], 0)
        product = lax.dot_general(
            left_operand(mine, scale),
            wide.reshape(-1, group).astype(jnp.bfloat16),
            (((1,), (0,)), ((), ())),
            preferred_element_type=jnp.float32,
        ).astype(jnp.bfloat16)
        for z in range(2):
            out[j, z] = product[z * group : (z + 1) * group]


def correlate_far(place, sources, first, slots, shape, result):
    in_specs = []
    operands = []
    group = shape[2]
    for source in sources:
        for part, starts, _ in source:
            skip = (first - starts) // STEP
            block = (part.shape[0], STEP) + part.shape[2:]
            in_specs.append(pl.BlockSpec(block, lambda j, place, skip=skip: (0, skip + j, 0, 0)))
            operands.append(part)
    counts = tuple(len(source) for source in sources)

    def kernel(*refs):
        correlate_far_kernel(counts, *refs)

    def column(j, place):
        return first // STEP + j, 0, 0, lax.rem(place[1] + 2, shape[3] // group)

    return pl.pallas_call(
        kernel,
        out_shape=jax.ShapeDtypeStruct(shape, jnp.bfloat16),
        grid_spec=pltpu.PrefetchScalarGridSpec(
            num_scalar_prefetch=1,
            grid=(slots // STEP,),
            in_specs=in_specs + [pl.BlockSpec(memory_space=pl.ANY)],
            out_specs=pl.BlockSpec((STEP, 2, group, group), column),
        ),
        input_output_aliases={len(operands) + 1: 0},
        compiler_params=pltpu.CompilerParams(
            dimension_semantics=("arbitrary",), vmem_limit_bytes=VMEM
        ),
        cost_estimate=pl.CostEstimate(flops=10**10, bytes_accessed=4 * 10**7, transcendentals=0),
        name="correlate_far",
    )(place, *operands, result)


def correlate_kernel(parts_of, place, *refs):
    out = refs[-1]
    me = place[1]
    group = out.shape[2]
    groups = out.shape[3] // group
    sources = []
    at = 0
    for count in parts_of:
        sources.append(refs[at : at + count])
        at += count
    scale = CORES / (2 * BLOCKS * refs[0].shape[0])
    for j in range(out.shape[0]):
        for ahead, source in zip(AHEAD, sources):
            wide = jnp.concatenate([gathered(piece, j) for piece in source], 0)
            if ahead == 0:
                lhs = left_operand(wide, scale)
            product = lax.dot_general(
                lhs,
                wide.reshape(-1, group).astype(jnp.bfloat16),
                (((1,), (0,)), ((), ())),
                preferred_element_type=jnp.float32,
            ).astype(jnp.bfloat16)
            at = pl.ds(pl.multiple_of(lax.rem(me + ahead, groups) * group, group), group)
            for z in range(2):
                out[j, z, :, at] = product[z * group : (z + 1) * group]


def correlate(place, sources, first, slots, shape, result):
    in_specs = []
    operands = []
    for ahead, source in zip(AHEAD, sources):
        for part, starts, axis in source:
            skip = (first - starts) // STEP
            if axis is None:
                block = (part.shape[0], STEP) + part.shape[2:]
            else:
                block = [None if k == axis else part.shape[k] for k in range(part.ndim)]
                block[2] = STEP
            groups = None if axis is None else part.shape[axis]

            def index(j, place, ahead=ahead, skip=skip, axis=axis, groups=groups):
                if axis is None:
                    return 0, skip + j, 0, 0
                which = lax.rem(place[1] + ahead, groups)
                return (which, 0, skip + j, 0, 0) if axis == 0 else (0, which, skip + j, 0, 0)

            in_specs.append(pl.BlockSpec(tuple(block), index))
            operands.append(part)
    parts_of = tuple(len(source) for source in sources)
    aliases = {}
    if result is not None:
        in_specs.append(pl.BlockSpec(memory_space=pl.ANY))
        aliases = {len(operands) + 1: 0}
        operands.append(result)

    def kernel(*refs):
        correlate_kernel(parts_of, *refs)

    return pl.pallas_call(
        kernel,
        out_shape=jax.ShapeDtypeStruct(shape, jnp.bfloat16),
        grid_spec=pltpu.PrefetchScalarGridSpec(
            num_scalar_prefetch=1,
            grid=(slots // STEP,),
            in_specs=in_specs,
            out_specs=pl.BlockSpec(
                (STEP,) + shape[1:], lambda j, place: (first // STEP + j, 0, 0, 0)
            ),
        ),
        input_output_aliases=aliases,
        compiler_params=pltpu.CompilerParams(
            dimension_semantics=("arbitrary",), vmem_limit_bytes=VMEM
        ),
        cost_estimate=pl.CostEstimate(flops=10**9, bytes_accessed=4 * 10**6, transcendentals=0),
        name="correlate",
    )(place, *operands)


def body(voltage, flags, owner_slot):
    owners = lax.axis_size("freq")
    groups = lax.axis_size("feed")
    chips = owners // CORES
    band = owner_slot.shape[0]
    feeds = voltage.shape[1]
    position = lax.axis_index("freq")
    place = jnp.stack(
        [position % CORES, lax.axis_index("feed"), (position >= CORES).astype(jnp.int32)]
    ).astype(jnp.int32)

    (given,) = pick(place, voltage, 1, voltage.shape[2])
    other = lax.ppermute(given, "freq", [(k, k ^ 1) for k in range(owners)])
    edges = pick(place, after(voltage, given), 2, 2 * CH)
    halo = []
    for k, edge in enumerate(edges):
        down = [(CORES * (c + 1), CORES * c + k) for c in range(chips - 1)]
        up = [(CORES * c + 1, CORES * ((c + 1) % chips) + 1 - k) for c in range(chips)]
        halo.append(lax.ppermute(edge, "freq", down + up))
    kept = flags[0].astype(jnp.float32) * (1.0 / math.sqrt(CH))
    slot = []
    first = 0
    for slots in PIECES:
        row = np.arange(owners * slots)
        slot.append(row // slots * CAP + first + row % slots)
        first += slots
    slot = jnp.asarray(np.concatenate(slot), jnp.int32)
    select = jnp.where(owner_slot[None, :] == slot[:, None], kept[None, :], 0.0)
    table = jnp.dot(
        select.astype(jnp.bfloat16), jnp.asarray(tables(band)), preferred_element_type=jnp.float32
    ).astype(jnp.bfloat16)

    def ring(value, steps):
        return lax.ppermute(value, "feed", [(k, (k + steps) % groups) for k in range(groups)])

    def exchanged(spectra):
        return lax.all_to_all(spectra, "freq", 0, 0, tiled=True)

    def far(left, right):
        middle = owners // 2
        return ring(left[:middle], 1), ring(right[middle:], -1)

    small, large = PIECES
    a0, a1 = channelize(place, after(voltage, *edges), other, (), table, EARLY, PIECES, PIECES, owners)
    left_a0, right_a0, far_a0 = ring(a0, 1), ring(a0, -1), ring(a0, 2)
    own_a1 = exchanged(a1)
    (b,) = channelize(place, voltage, other, tuple(halo), table, LATE, PIECES, (CAP,), owners)
    (b,) = channelize(place, voltage, other, tuple(halo), table, LATE, PIECES, (CAP,), owners)
    own_a1 = after(own_a1, b, left_a0, right_a0, far_a0)
    left_a1, right_a1 = ring(own_a1, 1), ring(own_a1, -1)
    far_a1 = far(left_a1, right_a1)
    own_b = exchanged(after(b, own_a1))
    all_a0 = pack((a0, left_a0, right_a0, far_a0), (left_a1, right_a1))
    own_b = after(own_b, all_a0)
    ready_b = after(own_b, *far_a1)
    own_b1 = ready_b[:, small:]
    own_b0 = ready_b[:, :small]
    left_b1, right_b1 = ring(own_b1, 1), ring(own_b1, -1)
    left_b0, right_b0 = ring(own_b0, 1), ring(own_b0, -1)
    all_a0 = exchanged(after(all_a0, ready_b))
    far_b1 = far(left_b1, right_b1)

    def whole(own, parts, first):
        return [[own]] + [
            [(part, first, None) for part in (group if isinstance(group, tuple) else (group,))]
            for group in parts
        ]

    shape = (CAP, 2, feeds, feeds * groups)
    early = whole((own_a1, small, None), (left_a1, right_a1, far_a1), small)
    late = whole((own_b, 0, None), (left_b1, right_b1, far_b1), small)
    sources = [one + two for one, two in zip(early, late)]
    result = correlate(place, sources[:3], small, large, shape, None)
    left_b0, right_b0, result = after_all((left_b0, right_b0, result), ())
    far_b0 = far(left_b0, right_b0)
    result = correlate_far(place, [sources[0], sources[3]], small, large, shape, result)
    late = whole((own_b, 0, None), (left_b0, right_b0, far_b0), 0)
    sources = [[(all_a0, -small * k, None)] + two for k, two in enumerate(late)]
    return correlate(place, sources, 0, small, shape, result)


def solution(mesh):
    placed = (P(None, "feed", "freq"), P("feed", None), P())
    return jax.shard_map(
        body, mesh=mesh, in_specs=placed, out_specs=P("freq", None, "feed", None), check_vma=False
    )
```

```python
import math

import jax
import jax.numpy as jnp
import ml_dtypes
import numpy as np
from jax import lax
from jax.experimental import pallas as pl
from jax.experimental.pallas import tpu as pltpu
from jax.sharding import PartitionSpec as P

CH = 1024
TAPS = 4
BAND_LO = 256
CAP = 20
CORES = 2
BLOCKS = 4
PIECES = (8, 12)
EARLY = ((0, 4),)
LATE = ((0, 1), (4, 3))
STEP = 4
AHEAD = (0, 3, 1, 2)
VMEM = 60 * 1024 * 1024
WEIGHT = pl.CostEstimate(flops=10**13, bytes_accessed=2 * 10**10, transcendentals=0)


def prototype():
    total = TAPS * CH
    position = np.arange(total).astype(np.float32)
    offset = (position - total / 2 + 0.5) / CH
    taper = 0.5 - 0.5 * np.cos(2 * np.pi * (position + 0.5) / total)
    coeffs = np.sinc(offset) * taper
    coeffs = coeffs * np.sqrt(CH / np.sum(coeffs * coeffs))
    return coeffs.reshape(TAPS, CH).astype(np.float32)


def tables(band):
    sample = np.arange(CH)
    channel = np.arange(band) + BAND_LO
    phase = (channel[:, None] * sample[None, :] % CH).astype(np.float32) * np.float32(2 * np.pi / CH)
    cosine = np.cos(phase).astype(ml_dtypes.bfloat16)
    sine = np.sin(phase).astype(ml_dtypes.bfloat16)
    return np.concatenate([cosine, sine], 1)


def after(value, *earlier):
    return lax.optimization_barrier((value,) + earlier)[0]


def after_all(values, earlier):
    return lax.optimization_barrier(tuple(values) + tuple(earlier))[: len(values)]


def pick_kernel(place, voltage, *rest):
    outs, sems = rest[:-1], rest[-1]
    core = place[0]
    half = voltage.shape[1] // CORES
    copies = []
    for k, out in enumerate(outs):
        width = out.shape[2]
        first = core * width if width < voltage.shape[2] else 0
        base = (1 - core if k + 1 == len(outs) else core) * half
        source = voltage.at[
            :, pl.ds(pl.multiple_of(base, half), half), pl.ds(pl.multiple_of(first, CH), width)
        ]
        copies.append(pltpu.make_async_copy(source, out, sems.at[k]))
    for copy in copies:
        copy.start()
    for copy in copies:
        copy.wait()


def pick(place, voltage, count, width):
    half = voltage.shape[1] // CORES
    return pl.pallas_call(
        pick_kernel,
        out_shape=[jax.ShapeDtypeStruct((2, half, width), jnp.bfloat16)] * count,
        in_specs=[pl.BlockSpec(memory_space=pltpu.SMEM), pl.BlockSpec(memory_space=pl.ANY)],
        out_specs=[pl.BlockSpec(memory_space=pltpu.VMEM)] * count,
        scratch_shapes=[pltpu.SemaphoreType.DMA((count,))],
        compiler_params=pltpu.CompilerParams(vmem_limit_bytes=VMEM),
        cost_estimate=WEIGHT,
        name="pick",
    )(place, voltage)


def channelize_kernel(windows, pieces, place, voltage, other, *rest):
    second = len(windows) == 2
    halo = rest[: 2 * second]
    rest = rest[2 * second :]
    coeffs, table = rest[:2]
    outs = rest[2:-5]
    held, weighted, chosen, spread, sems = rest[-5:]
    core = place[0]
    half = voltage.shape[1] // CORES
    own_rows = pl.ds(pl.multiple_of(core * half, half), half)
    tail = TAPS - 1
    fetch = pltpu.make_async_copy(table, chosen, sems.at[4])
    fetch.start()

    def load(parts):
        copies = []
        for source, first, count, at in parts:
            if source is voltage:
                block = voltage.at[:, own_rows, pl.ds(first * CH, count * CH)]
            else:
                block = source.at[:, :, pl.ds(first * CH, count * CH)]
            target = held.at[:, :, pl.ds(at * CH, count * CH)]
            copies.append(pltpu.make_async_copy(block, target, sems.at[len(copies)]))
        for copy in copies:
            copy.start()
        for copy in copies:
            copy.wait()

    def load_for(low, high, nearer):
        if second:
            previous, following = nearer
            load(
                [
                    (previous, 1, 1, 0),
                    (low, 0, tail, 1),
                    (high, 0, BLOCKS, BLOCKS),
                    (following, 0, 2, 2 * BLOCKS),
                ]
            )
        else:
            load([(low, 0, BLOCKS, 0), (high, 0, tail, BLOCKS)])

    @pl.when(core == 0)
    def _():
        load_for(voltage, other, halo[::-1])

    @pl.when(core != 0)
    def _():
        load_for(other, voltage, halo)

    keep = place[2].astype(jnp.float32)
    rows = 16
    width = 256

    def step(index, carry):
        at = pl.ds(pl.multiple_of(index * rows, rows), rows)
        for z in range(2):
            for start in range(0, CH, width):
                taps = [coeffs[p : p + 1, pl.ds(start, width)] for p in range(TAPS)]
                s = 0
                for window, (base, count) in enumerate(windows):
                    blocks = [
                        held[z, at, pl.ds((base + b) * CH + start, width)].astype(jnp.float32)
                        for b in range(count + TAPS - 1)
                    ]
                    for k in range(count):
                        total = blocks[k] * taps[0]
                        for p in range(1, TAPS):
                            tap = taps[p] * keep if second and window == 0 else taps[p]
                            total = total + blocks[k + p] * tap
                        weighted[z, s, at, pl.ds(start, width)] = total.astype(jnp.bfloat16)
                        s += 1
        return carry

    lax.fori_loop(0, half // rows, step, 0)
    fetch.wait()
    owners = outs[0].shape[0]
    places = [(out, j) for out in outs for j in range(out.shape[1])]
    columns = BLOCKS * half
    samples = weighted[...].reshape(2 * columns, CH)
    base = 0
    for slots in pieces:
        number = owners * slots
        at = pl.ds(base, number)
        out, first = places[base // owners]
        both = jnp.concatenate([chosen[at, :CH], chosen[at, CH:]], 0)
        product = lax.dot_general(
            both, samples, (((1,), (1,)), ((), ())), preferred_element_type=jnp.float32
        )
        parts = (
            product[:number, :columns] + product[number:, columns:],
            product[:number, columns:] - product[number:, :columns],
        )
        for z in range(2):
            for s in range(BLOCKS):
                spread[pl.ds(z * BLOCKS + s, number, stride=2 * BLOCKS), :] = parts[z][
                    :, s * half : (s + 1) * half
                ]
        out[:, first : first + slots] = (
            spread[pl.ds(0, number * 2 * BLOCKS), :]
            .reshape(owners, slots, 2 * BLOCKS, half)
            .astype(jnp.bfloat16)
        )
        base += number


def channelize(place, voltage, other, halo, table, windows, pieces, sent, owners):
    half = voltage.shape[1] // CORES
    operands = (voltage, other) + halo
    span = sum(count + TAPS - 1 for _, count in windows)
    anywhere = pl.BlockSpec(memory_space=pl.ANY)
    vmem = pl.BlockSpec(memory_space=pltpu.VMEM)

    def kernel(*refs):
        channelize_kernel(windows, pieces, *refs)

    return pl.pallas_call(
        kernel,
        out_shape=[
            jax.ShapeDtypeStruct((owners, slots, 2 * BLOCKS, half), jnp.bfloat16)
            for slots in sent
        ],
        in_specs=[pl.BlockSpec(memory_space=pltpu.SMEM)]
        + [anywhere] * len(operands)
        + [vmem, anywhere],
        out_specs=[vmem] * len(sent),
        scratch_shapes=[
            pltpu.VMEM((2, half, span * CH), jnp.bfloat16),
            pltpu.VMEM((2, BLOCKS, half, CH), jnp.bfloat16),
            pltpu.VMEM(table.shape, jnp.bfloat16),
            pltpu.VMEM((owners * max(pieces) * 2 * BLOCKS, half), jnp.float32),
            pltpu.SemaphoreType.DMA((5,)),
        ],
        compiler_params=pltpu.CompilerParams(vmem_limit_bytes=VMEM),
        cost_estimate=WEIGHT,
        name="channelize",
    )(place, *operands, jnp.asarray(prototype()), table)


def pack_kernel(*refs):
    out = refs[-1]
    slots = refs[0].shape[1]
    for k, ref in enumerate(refs[:4]):
        out[:, k * slots : (k + 1) * slots] = ref[...]


def pack(parts, wait):
    count, slots, rows, lanes = parts[0].shape
    step = count // 8
    block = pl.BlockSpec((step, slots, rows, lanes), lambda k: (k, 0, 0, 0))
    return pl.pallas_call(
        pack_kernel,
        grid=(count // step,),
        out_shape=jax.ShapeDtypeStruct((count, len(parts) * slots, rows, lanes), jnp.bfloat16),
        in_specs=[block] * len(parts),
        out_specs=pl.BlockSpec((step, len(parts) * slots, rows, lanes), lambda k: (k, 0, 0, 0)),
        compiler_params=pltpu.CompilerParams(
            dimension_semantics=("arbitrary",), vmem_limit_bytes=VMEM
        ),
        cost_estimate=WEIGHT,
        name="pack",
    )(*after_all(parts, wait))


def gathered(part, j):
    count, _, rows, lanes = part.shape
    wide = part[:, j].astype(jnp.float32).reshape(count // CORES, CORES, rows, lanes)
    return jnp.concatenate([wide[:, core] for core in range(CORES)], 2)


def left_operand(mine, scale):
    group = mine.shape[2]
    row = lax.broadcasted_iota(jnp.int32, (1, 2 * BLOCKS, group), 1)
    sign = jnp.where(row < BLOCKS, -1.0, 1.0)
    mine = mine * scale
    turned = pltpu.roll(mine, BLOCKS, 1) * sign
    both = jnp.concatenate([mine, turned], 2)
    return jnp.transpose(both.reshape(-1, 2 * group).astype(jnp.bfloat16))


def correlate_far_kernel(counts, place, *refs):
    out = refs[-1]
    group = out.shape[2]
    own, far = refs[: counts[0]], refs[counts[0] : sum(counts)]
    scale = CORES / (2 * BLOCKS * refs[0].shape[0])
    for j in range(out.shape[0]):
        mine = jnp.concatenate([gathered(piece, j) for piece in own], 0)
        wide = jnp.concatenate([gathered(piece, j) for piece in far], 0)
        product = lax.dot_general(
            left_operand(mine, scale),
            wide.reshape(-1, group).astype(jnp.bfloat16),
            (((1,), (0,)), ((), ())),
            preferred_element_type=jnp.float32,
        ).astype(jnp.bfloat16)
        for z in range(2):
            out[j, z] = product[z * group : (z + 1) * group]


def correlate_far(place, sources, first, slots, shape, result):
    in_specs = []
    operands = []
    group = shape[2]
    for source in sources:
        for part, starts, _ in source:
            skip = (first - starts) // STEP
            block = (part.shape[0], STEP) + part.shape[2:]
            in_specs.append(pl.BlockSpec(block, lambda j, place, skip=skip: (0, skip + j, 0, 0)))
            operands.append(part)
    counts = tuple(len(source) for source in sources)

    def kernel(*refs):
        correlate_far_kernel(counts, *refs)

    def column(j, place):
        return first // STEP + j, 0, 0, lax.rem(place[1] + 2, shape[3] // group)

    return pl.pallas_call(
        kernel,
        out_shape=jax.ShapeDtypeStruct(shape, jnp.bfloat16),
        grid_spec=pltpu.PrefetchScalarGridSpec(
            num_scalar_prefetch=1,
            grid=(slots // STEP,),
            in_specs=in_specs + [pl.BlockSpec(memory_space=pl.ANY)],
            out_specs=pl.BlockSpec((STEP, 2, group, group), column),
        ),
        input_output_aliases={len(operands) + 1: 0},
        compiler_params=pltpu.CompilerParams(
            dimension_semantics=("arbitrary",), vmem_limit_bytes=VMEM
        ),
        cost_estimate=pl.CostEstimate(flops=10**10, bytes_accessed=4 * 10**7, transcendentals=0),
        name="correlate_far",
    )(place, *operands, result)


def correlate_kernel(parts_of, place, *refs):
    out = refs[-1]
    me = place[1]
    group = out.shape[2]
    groups = out.shape[3] // group
    sources = []
    at = 0
    for count in parts_of:
        sources.append(refs[at : at + count])
        at += count
    scale = CORES / (2 * BLOCKS * refs[0].shape[0])
    for j in range(out.shape[0]):
        for ahead, source in zip(AHEAD, sources):
            wide = jnp.concatenate([gathered(piece, j) for piece in source], 0)
            if ahead == 0:
                lhs = left_operand(wide, scale)
            product = lax.dot_general(
                lhs,
                wide.reshape(-1, group).astype(jnp.bfloat16),
                (((1,), (0,)), ((), ())),
                preferred_element_type=jnp.float32,
            ).astype(jnp.bfloat16)
            at = pl.ds(pl.multiple_of(lax.rem(me + ahead, groups) * group, group), group)
            for z in range(2):
                out[j, z, :, at] = product[z * group : (z + 1) * group]


def correlate(place, sources, first, slots, shape, result):
    in_specs = []
    operands = []
    for ahead, source in zip(AHEAD, sources):
        for part, starts, axis in source:
            skip = (first - starts) // STEP
            if axis is None:
                block = (part.shape[0], STEP) + part.shape[2:]
            else:
                block = [None if k == axis else part.shape[k] for k in range(part.ndim)]
                block[2] = STEP
            groups = None if axis is None else part.shape[axis]

            def index(j, place, ahead=ahead, skip=skip, axis=axis, groups=groups):
                if axis is None:
                    return 0, skip + j, 0, 0
                which = lax.rem(place[1] + ahead, groups)
                return (which, 0, skip + j, 0, 0) if axis == 0 else (0, which, skip + j, 0, 0)

            in_specs.append(pl.BlockSpec(tuple(block), index))
            operands.append(part)
    parts_of = tuple(len(source) for source in sources)
    aliases = {}
    if result is not None:
        in_specs.append(pl.BlockSpec(memory_space=pl.ANY))
        aliases = {len(operands) + 1: 0}
        operands.append(result)

    def kernel(*refs):
        correlate_kernel(parts_of, *refs)

    return pl.pallas_call(
        kernel,
        out_shape=jax.ShapeDtypeStruct(shape, jnp.bfloat16),
        grid_spec=pltpu.PrefetchScalarGridSpec(
            num_scalar_prefetch=1,
            grid=(slots // STEP,),
            in_specs=in_specs,
            out_specs=pl.BlockSpec(
                (STEP,) + shape[1:], lambda j, place: (first // STEP + j, 0, 0, 0)
            ),
        ),
        input_output_aliases=aliases,
        compiler_params=pltpu.CompilerParams(
            dimension_semantics=("arbitrary",), vmem_limit_bytes=VMEM
        ),
        cost_estimate=pl.CostEstimate(flops=10**9, bytes_accessed=4 * 10**6, transcendentals=0),
        name="correlate",
    )(place, *operands)


def body(voltage, flags, owner_slot):
    owners = lax.axis_size("freq")
    groups = lax.axis_size("feed")
    chips = owners // CORES
    band = owner_slot.shape[0]
    feeds = voltage.shape[1]
    position = lax.axis_index("freq")
    place = jnp.stack(
        [position % CORES, lax.axis_index("feed"), (position >= CORES).astype(jnp.int32)]
    ).astype(jnp.int32)

    (given,) = pick(place, voltage, 1, voltage.shape[2])
    other = lax.ppermute(given, "freq", [(k, k ^ 1) for k in range(owners)])
    edges = pick(place, after(voltage, given), 2, 2 * CH)
    halo = []
    for k, edge in enumerate(edges):
        down = [(CORES * (c + 1), CORES * c + k) for c in range(chips - 1)]
        up = [(CORES * c + 1, CORES * ((c + 1) % chips) + 1 - k) for c in range(chips)]
        halo.append(lax.ppermute(edge, "freq", down + up))
    kept = flags[0].astype(jnp.float32) * (1.0 / math.sqrt(CH))
    slot = []
    first = 0
    for slots in PIECES:
        row = np.arange(owners * slots)
        slot.append(row // slots * CAP + first + row % slots)
        first += slots
    slot = jnp.asarray(np.concatenate(slot), jnp.int32)
    select = jnp.where(owner_slot[None, :] == slot[:, None], kept[None, :], 0.0)
    table = jnp.dot(
        select.astype(jnp.bfloat16), jnp.asarray(tables(band)), preferred_element_type=jnp.float32
    ).astype(jnp.bfloat16)

    def ring(value, steps):
        return lax.ppermute(value, "feed", [(k, (k + steps) % groups) for k in range(groups)])

    def exchanged(spectra):
        return lax.all_to_all(spectra, "freq", 0, 0, tiled=True)

    def far(left, right):
        middle = owners // 2
        return ring(left[:middle], 1), ring(right[middle:], -1)

    small, large = PIECES
    a0, a1 = channelize(place, after(voltage, *edges), other, (), table, EARLY, PIECES, PIECES, owners)
    left_a0, right_a0, far_a0 = ring(a0, 1), ring(a0, -1), ring(a0, 2)
    own_a1 = exchanged(a1)
    (b,) = channelize(place, voltage, other, tuple(halo), table, LATE, PIECES, (CAP,), owners)
    (b,) = channelize(place, voltage, other, tuple(halo), table, LATE, PIECES, (CAP,), owners)
    own_a1 = after(own_a1, b, left_a0, right_a0, far_a0)
    left_a1, right_a1 = ring(own_a1, 1), ring(own_a1, -1)
    far_a1 = far(left_a1, right_a1)
    own_b = exchanged(after(b, own_a1))
    all_a0 = pack((a0, left_a0, right_a0, far_a0), (left_a1, right_a1))
    own_b = after(own_b, all_a0)
    own_b1 = after(own_b[:, small:], *far_a1)
    own_b0 = after(own_b[:, :small], *far_a1)
    left_b1, right_b1 = ring(own_b1, 1), ring(own_b1, -1)
    left_b0, right_b0 = ring(own_b0, 1), ring(own_b0, -1)
    all_a0 = exchanged(after(all_a0, own_b1))
    far_b1 = far(left_b1, right_b1)

    def whole(own, parts, first):
        return [[own]] + [
            [(part, first, None) for part in (group if isinstance(group, tuple) else (group,))]
            for group in parts
        ]

    shape = (CAP, 2, feeds, feeds * groups)
    early = whole((own_a1, small, None), (left_a1, right_a1, far_a1), small)
    late = whole((own_b, 0, None), (left_b1, right_b1, far_b1), small)
    sources = [one + two for one, two in zip(early, late)]
    result = correlate(place, sources[:3], small, large, shape, None)
    left_b0, right_b0, result = after_all((left_b0, right_b0, result), ())
    far_b0 = far(left_b0, right_b0)
    result = correlate_far(place, [sources[0], sources[3]], small, large, shape, result)
    late = whole((own_b, 0, None), (left_b0, right_b0, far_b0), 0)
    sources = [[(all_a0, -small * k, None)] + two for k, two in enumerate(late)]
    return correlate(place, sources, 0, small, shape, result)


def solution(mesh):
    placed = (P(None, "feed", "freq"), P("feed", None), P())
    return jax.shard_map(
        body, mesh=mesh, in_specs=placed, out_specs=P("freq", None, "feed", None), check_vma=False
    )
```

```python
import math

import jax
import jax.numpy as jnp
import ml_dtypes
import numpy as np
from jax import lax
from jax.experimental import pallas as pl
from jax.experimental.pallas import tpu as pltpu
from jax.sharding import PartitionSpec as P

CH = 1024
TAPS = 4
BAND_LO = 256
CAP = 20
CORES = 2
BLOCKS = 4
PIECES = (8, 12)
EARLY = ((0, 4),)
LATE = ((0, 1), (4, 3))
STEP = 4
AHEAD = (0, 3, 1, 2)
VMEM = 60 * 1024 * 1024
WEIGHT = pl.CostEstimate(flops=10**13, bytes_accessed=2 * 10**10, transcendentals=0)


def prototype():
    total = TAPS * CH
    position = np.arange(total).astype(np.float32)
    offset = (position - total / 2 + 0.5) / CH
    taper = 0.5 - 0.5 * np.cos(2 * np.pi * (position + 0.5) / total)
    coeffs = np.sinc(offset) * taper
    coeffs = coeffs * np.sqrt(CH / np.sum(coeffs * coeffs))
    return coeffs.reshape(TAPS, CH).astype(np.float32)


def tables(band):
    sample = np.arange(CH)
    channel = np.arange(band) + BAND_LO
    phase = (channel[:, None] * sample[None, :] % CH).astype(np.float32) * np.float32(2 * np.pi / CH)
    cosine = np.cos(phase).astype(ml_dtypes.bfloat16)
    sine = np.sin(phase).astype(ml_dtypes.bfloat16)
    return np.concatenate([cosine, sine], 1)


def after(value, *earlier):
    return lax.optimization_barrier((value,) + earlier)[0]


def after_all(values, earlier):
    return lax.optimization_barrier(tuple(values) + tuple(earlier))[: len(values)]


def pick_kernel(place, voltage, *rest):
    outs, sems = rest[:-1], rest[-1]
    core = place[0]
    half = voltage.shape[1] // CORES
    copies = []
    for k, out in enumerate(outs):
        width = out.shape[2]
        first = core * width if width < voltage.shape[2] else 0
        base = (1 - core if k + 1 == len(outs) else core) * half
        source = voltage.at[
            :, pl.ds(pl.multiple_of(base, half), half), pl.ds(pl.multiple_of(first, CH), width)
        ]
        copies.append(pltpu.make_async_copy(source, out, sems.at[k]))
    for copy in copies:
        copy.start()
    for copy in copies:
        copy.wait()


def pick(place, voltage, count, width):
    half = voltage.shape[1] // CORES
    return pl.pallas_call(
        pick_kernel,
        out_shape=[jax.ShapeDtypeStruct((2, half, width), jnp.bfloat16)] * count,
        in_specs=[pl.BlockSpec(memory_space=pltpu.SMEM), pl.BlockSpec(memory_space=pl.ANY)],
        out_specs=[pl.BlockSpec(memory_space=pltpu.VMEM)] * count,
        scratch_shapes=[pltpu.SemaphoreType.DMA((count,))],
        compiler_params=pltpu.CompilerParams(vmem_limit_bytes=VMEM),
        cost_estimate=WEIGHT,
        name="pick",
    )(place, voltage)


def channelize_kernel(windows, pieces, place, voltage, other, *rest):
    second = len(windows) == 2
    halo = rest[: 2 * second]
    rest = rest[2 * second :]
    coeffs, table = rest[:2]
    outs = rest[2:-5]
    held, weighted, chosen, spread, sems = rest[-5:]
    core = place[0]
    half = voltage.shape[1] // CORES
    own_rows = pl.ds(pl.multiple_of(core * half, half), half)
    tail = TAPS - 1
    fetch = pltpu.make_async_copy(table, chosen, sems.at[4])
    fetch.start()

    def load(parts):
        copies = []
        for source, first, count, at in parts:
            if source is voltage:
                block = voltage.at[:, own_rows, pl.ds(first * CH, count * CH)]
            else:
                block = source.at[:, :, pl.ds(first * CH, count * CH)]
            target = held.at[:, :, pl.ds(at * CH, count * CH)]
            copies.append(pltpu.make_async_copy(block, target, sems.at[len(copies)]))
        for copy in copies:
            copy.start()
        for copy in copies:
            copy.wait()

    def load_for(low, high, nearer):
        if second:
            previous, following = nearer
            load(
                [
                    (previous, 1, 1, 0),
                    (low, 0, tail, 1),
                    (high, 0, BLOCKS, BLOCKS),
                    (following, 0, 2, 2 * BLOCKS),
                ]
            )
        else:
            load([(low, 0, BLOCKS, 0), (high, 0, tail, BLOCKS)])

    @pl.when(core == 0)
    def _():
        load_for(voltage, other, halo[::-1])

    @pl.when(core != 0)
    def _():
        load_for(other, voltage, halo)

    keep = place[2].astype(jnp.float32)
    rows = 16
    width = 256

    def step(index, carry):
        at = pl.ds(pl.multiple_of(index * rows, rows), rows)
        for z in range(2):
            for start in range(0, CH, width):
                taps = [coeffs[p : p + 1, pl.ds(start, width)] for p in range(TAPS)]
                s = 0
                for window, (base, count) in enumerate(windows):
                    blocks = [
                        held[z, at, pl.ds((base + b) * CH + start, width)].astype(jnp.float32)
                        for b in range(count + TAPS - 1)
                    ]
                    for k in range(count):
                        total = blocks[k] * taps[0]
                        for p in range(1, TAPS):
                            tap = taps[p] * keep if second and window == 0 else taps[p]
                            total = total + blocks[k + p] * tap
                        weighted[z, s, at, pl.ds(start, width)] = total.astype(jnp.bfloat16)
                        s += 1
        return carry

    lax.fori_loop(0, half // rows, step, 0)
    fetch.wait()
    owners = outs[0].shape[0]
    places = [(out, j) for out in outs for j in range(out.shape[1])]
    columns = BLOCKS * half
    samples = weighted[...].reshape(2 * columns, CH)
    base = 0
    for slots in pieces:
        number = owners * slots
        at = pl.ds(base, number)
        out, first = places[base // owners]
        both = jnp.concatenate([chosen[at, :CH], chosen[at, CH:]], 0)
        product = lax.dot_general(
            both, samples, (((1,), (1,)), ((), ())), preferred_element_type=jnp.float32
        )
        parts = (
            product[:number, :columns] + product[number:, columns:],
            product[:number, columns:] - product[number:, :columns],
        )
        for z in range(2):
            for s in range(BLOCKS):
                spread[pl.ds(z * BLOCKS + s, number, stride=2 * BLOCKS), :] = parts[z][
                    :, s * half : (s + 1) * half
                ]
        out[:, first : first + slots] = (
            spread[pl.ds(0, number * 2 * BLOCKS), :]
            .reshape(owners, slots, 2 * BLOCKS, half)
            .astype(jnp.bfloat16)
        )
        base += number


def channelize(place, voltage, other, halo, table, windows, pieces, sent, owners):
    half = voltage.shape[1] // CORES
    operands = (voltage, other) + halo
    span = sum(count + TAPS - 1 for _, count in windows)
    anywhere = pl.BlockSpec(memory_space=pl.ANY)
    vmem = pl.BlockSpec(memory_space=pltpu.VMEM)

    def kernel(*refs):
        channelize_kernel(windows, pieces, *refs)

    return pl.pallas_call(
        kernel,
        out_shape=[
            jax.ShapeDtypeStruct((owners, slots, 2 * BLOCKS, half), jnp.bfloat16)
            for slots in sent
        ],
        in_specs=[pl.BlockSpec(memory_space=pltpu.SMEM)]
        + [anywhere] * len(operands)
        + [vmem, anywhere],
        out_specs=[vmem] * len(sent),
        scratch_shapes=[
            pltpu.VMEM((2, half, span * CH), jnp.bfloat16),
            pltpu.VMEM((2, BLOCKS, half, CH), jnp.bfloat16),
            pltpu.VMEM(table.shape, jnp.bfloat16),
            pltpu.VMEM((owners * max(pieces) * 2 * BLOCKS, half), jnp.float32),
            pltpu.SemaphoreType.DMA((5,)),
        ],
        compiler_params=pltpu.CompilerParams(vmem_limit_bytes=VMEM),
        cost_estimate=WEIGHT,
        name="channelize",
    )(place, *operands, jnp.asarray(prototype()), table)


def pack_kernel(*refs):
    out = refs[-1]
    slots = refs[0].shape[1]
    for k, ref in enumerate(refs[:4]):
        out[:, k * slots : (k + 1) * slots] = ref[...]


def pack(parts, wait):
    count, slots, rows, lanes = parts[0].shape
    step = count // 8
    block = pl.BlockSpec((step, slots, rows, lanes), lambda k: (k, 0, 0, 0))
    return pl.pallas_call(
        pack_kernel,
        grid=(count // step,),
        out_shape=jax.ShapeDtypeStruct((count, len(parts) * slots, rows, lanes), jnp.bfloat16),
        in_specs=[block] * len(parts),
        out_specs=pl.BlockSpec((step, len(parts) * slots, rows, lanes), lambda k: (k, 0, 0, 0)),
        compiler_params=pltpu.CompilerParams(
            dimension_semantics=("arbitrary",), vmem_limit_bytes=VMEM
        ),
        cost_estimate=WEIGHT,
        name="pack",
    )(*after_all(parts, wait))


def gathered(part, j):
    count, _, rows, lanes = part.shape
    wide = part[:, j].astype(jnp.float32).reshape(count // CORES, CORES, rows, lanes)
    return jnp.concatenate([wide[:, core] for core in range(CORES)], 2)


def left_operand(mine, scale):
    group = mine.shape[2]
    row = lax.broadcasted_iota(jnp.int32, (1, 2 * BLOCKS, group), 1)
    sign = jnp.where(row < BLOCKS, -1.0, 1.0)
    mine = mine * scale
    turned = pltpu.roll(mine, BLOCKS, 1) * sign
    both = jnp.concatenate([mine, turned], 2)
    return jnp.transpose(both.reshape(-1, 2 * group).astype(jnp.bfloat16))


def correlate_far_kernel(counts, place, *refs):
    out = refs[-1]
    group = out.shape[2]
    own, far = refs[: counts[0]], refs[counts[0] : sum(counts)]
    scale = CORES / (2 * BLOCKS * refs[0].shape[0])
    for j in range(out.shape[0]):
        mine = jnp.concatenate([gathered(piece, j) for piece in own], 0)
        wide = jnp.concatenate([gathered(piece, j) for piece in far], 0)
        product = lax.dot_general(
            left_operand(mine, scale),
            wide.reshape(-1, group).astype(jnp.bfloat16),
            (((1,), (0,)), ((), ())),
            preferred_element_type=jnp.float32,
        ).astype(jnp.bfloat16)
        for z in range(2):
            out[j, z] = product[z * group : (z + 1) * group]


def correlate_far(place, sources, first, slots, shape, result):
    in_specs = []
    operands = []
    group = shape[2]
    for source in sources:
        for part, starts, _ in source:
            skip = (first - starts) // STEP
            block = (part.shape[0], STEP) + part.shape[2:]
            in_specs.append(pl.BlockSpec(block, lambda j, place, skip=skip: (0, skip + j, 0, 0)))
            operands.append(part)
    counts = tuple(len(source) for source in sources)

    def kernel(*refs):
        correlate_far_kernel(counts, *refs)

    def column(j, place):
        return first // STEP + j, 0, 0, lax.rem(place[1] + 2, shape[3] // group)

    return pl.pallas_call(
        kernel,
        out_shape=jax.ShapeDtypeStruct(shape, jnp.bfloat16),
        grid_spec=pltpu.PrefetchScalarGridSpec(
            num_scalar_prefetch=1,
            grid=(slots // STEP,),
            in_specs=in_specs + [pl.BlockSpec(memory_space=pl.ANY)],
            out_specs=pl.BlockSpec((STEP, 2, group, group), column),
        ),
        input_output_aliases={len(operands) + 1: 0},
        compiler_params=pltpu.CompilerParams(
            dimension_semantics=("arbitrary",), vmem_limit_bytes=VMEM // 2
        ),
        cost_estimate=pl.CostEstimate(flops=10**10, bytes_accessed=4 * 10**7, transcendentals=0),
        name="correlate_far",
    )(place, *operands, result)


def correlate_kernel(parts_of, place, *refs):
    out = refs[-1]
    me = place[1]
    group = out.shape[2]
    groups = out.shape[3] // group
    sources = []
    at = 0
    for count in parts_of:
        sources.append(refs[at : at + count])
        at += count
    scale = CORES / (2 * BLOCKS * refs[0].shape[0])
    for j in range(out.shape[0]):
        for ahead, source in zip(AHEAD, sources):
            wide = jnp.concatenate([gathered(piece, j) for piece in source], 0)
            if ahead == 0:
                lhs = left_operand(wide, scale)
            product = lax.dot_general(
                lhs,
                wide.reshape(-1, group).astype(jnp.bfloat16),
                (((1,), (0,)), ((), ())),
                preferred_element_type=jnp.float32,
            ).astype(jnp.bfloat16)
            at = pl.ds(pl.multiple_of(lax.rem(me + ahead, groups) * group, group), group)
            for z in range(2):
                out[j, z, :, at] = product[z * group : (z + 1) * group]


def correlate(place, sources, first, slots, shape, result):
    in_specs = []
    operands = []
    for ahead, source in zip(AHEAD, sources):
        for part, starts, axis in source:
            skip = (first - starts) // STEP
            if axis is None:
                block = (part.shape[0], STEP) + part.shape[2:]
            else:
                block = [None if k == axis else part.shape[k] for k in range(part.ndim)]
                block[2] = STEP
            groups = None if axis is None else part.shape[axis]

            def index(j, place, ahead=ahead, skip=skip, axis=axis, groups=groups):
                if axis is None:
                    return 0, skip + j, 0, 0
                which = lax.rem(place[1] + ahead, groups)
                return (which, 0, skip + j, 0, 0) if axis == 0 else (0, which, skip + j, 0, 0)

            in_specs.append(pl.BlockSpec(tuple(block), index))
            operands.append(part)
    parts_of = tuple(len(source) for source in sources)
    aliases = {}
    if result is not None:
        in_specs.append(pl.BlockSpec(memory_space=pl.ANY))
        aliases = {len(operands) + 1: 0}
        operands.append(result)

    def kernel(*refs):
        correlate_kernel(parts_of, *refs)

    return pl.pallas_call(
        kernel,
        out_shape=jax.ShapeDtypeStruct(shape, jnp.bfloat16),
        grid_spec=pltpu.PrefetchScalarGridSpec(
            num_scalar_prefetch=1,
            grid=(slots // STEP,),
            in_specs=in_specs,
            out_specs=pl.BlockSpec(
                (STEP,) + shape[1:], lambda j, place: (first // STEP + j, 0, 0, 0)
            ),
        ),
        input_output_aliases=aliases,
        compiler_params=pltpu.CompilerParams(
            dimension_semantics=("arbitrary",), vmem_limit_bytes=VMEM // 2
        ),
        cost_estimate=pl.CostEstimate(flops=10**9, bytes_accessed=4 * 10**6, transcendentals=0),
        name="correlate",
    )(place, *operands)


def body(voltage, flags, owner_slot):
    owners = lax.axis_size("freq")
    groups = lax.axis_size("feed")
    chips = owners // CORES
    band = owner_slot.shape[0]
    feeds = voltage.shape[1]
    position = lax.axis_index("freq")
    place = jnp.stack(
        [position % CORES, lax.axis_index("feed"), (position >= CORES).astype(jnp.int32)]
    ).astype(jnp.int32)

    (given,) = pick(place, voltage, 1, voltage.shape[2])
    other = lax.ppermute(given, "freq", [(k, k ^ 1) for k in range(owners)])
    edges = pick(place, after(voltage, given), 2, 2 * CH)
    halo = []
    for k, edge in enumerate(edges):
        down = [(CORES * (c + 1), CORES * c + k) for c in range(chips - 1)]
        up = [(CORES * c + 1, CORES * ((c + 1) % chips) + 1 - k) for c in range(chips)]
        halo.append(lax.ppermute(edge, "freq", down + up))
    kept = flags[0].astype(jnp.float32) * (1.0 / math.sqrt(CH))
    slot = []
    first = 0
    for slots in PIECES:
        row = np.arange(owners * slots)
        slot.append(row // slots * CAP + first + row % slots)
        first += slots
    slot = jnp.asarray(np.concatenate(slot), jnp.int32)
    select = jnp.where(owner_slot[None, :] == slot[:, None], kept[None, :], 0.0)
    table = jnp.dot(
        select.astype(jnp.bfloat16), jnp.asarray(tables(band)), preferred_element_type=jnp.float32
    ).astype(jnp.bfloat16)

    def ring(value, steps):
        return lax.ppermute(value, "feed", [(k, (k + steps) % groups) for k in range(groups)])

    def exchanged(spectra):
        return lax.all_to_all(spectra, "freq", 0, 0, tiled=True)

    def far(left, right):
        middle = owners // 2
        return ring(left[:middle], 1), ring(right[middle:], -1)

    small, large = PIECES
    a0, a1 = channelize(place, after(voltage, *edges), other, (), table, EARLY, PIECES, PIECES, owners)
    left_a0, right_a0, far_a0 = ring(a0, 1), ring(a0, -1), ring(a0, 2)
    own_a1 = exchanged(a1)
    (b,) = channelize(place, voltage, other, tuple(halo), table, LATE, PIECES, (CAP,), owners)
    (b,) = channelize(place, voltage, other, tuple(halo), table, LATE, PIECES, (CAP,), owners)
    own_a1 = after(own_a1, b, left_a0, right_a0, far_a0)
    left_a1, right_a1 = ring(own_a1, 1), ring(own_a1, -1)
    far_a1 = far(left_a1, right_a1)
    own_b = exchanged(after(b, own_a1))
    all_a0 = pack((a0, left_a0, right_a0, far_a0), (left_a1, right_a1))
    own_b = after(own_b, all_a0)
    own_b1 = after(own_b[:, small:], *far_a1)
    own_b0 = after(own_b[:, :small], *far_a1)
    left_b1, right_b1 = ring(own_b1, 1), ring(own_b1, -1)
    left_b0, right_b0 = ring(own_b0, 1), ring(own_b0, -1)
    all_a0 = exchanged(after(all_a0, own_b1))
    far_b1 = far(left_b1, right_b1)

    def whole(own, parts, first):
        return [[own]] + [
            [(part, first, None) for part in (group if isinstance(group, tuple) else (group,))]
            for group in parts
        ]

    shape = (CAP, 2, feeds, feeds * groups)
    early = whole((own_a1, small, None), (left_a1, right_a1, far_a1), small)
    late = whole((own_b, 0, None), (left_b1, right_b1, far_b1), small)
    sources = [one + two for one, two in zip(early, late)]
    result = correlate(place, sources[:3], small, large, shape, None)
    left_b0, right_b0, result = after_all((left_b0, right_b0, result), ())
    far_b0 = far(left_b0, right_b0)
    result = correlate_far(place, [sources[0], sources[3]], small, large, shape, result)
    late = whole((own_b, 0, None), (left_b0, right_b0, far_b0), 0)
    sources = [[(all_a0, -small * k, None)] + two for k, two in enumerate(late)]
    return correlate(place, sources, 0, small, shape, result)


def solution(mesh):
    placed = (P(None, "feed", "freq"), P("feed", None), P())
    return jax.shard_map(
        body, mesh=mesh, in_specs=placed, out_specs=P("freq", None, "feed", None), check_vma=False
    )
```
